128 devices in a mesh: gx: 32 (over y, z, core), gy: 4 (over x).
Axes of the slice: x: 4, y: 4, z: 4, core: 2. Of those that a mesh axis runs over, the one named last changes fastest.
Arguments:
- right_side: float32 [4, 24, 768, 512], P(None, None, 'gx', 'gy'), may hold values from -8 to 8
- start_field: float32 [4, 24, 768, 512], P(None, None, 'gx', 'gy'), may hold values from -4 to 4
- center: float32 [24, 768, 512], P(None, 'gx', 'gy'), may hold values from 0.5 to 3
- weights: float32 [6, 24, 768, 512], P(None, None, 'gx', 'gy'), may hold values from 0.4 to 1.4
Outputs:
- solution: float32 [4, 24, 768, 512], P(None, None, 'gx', 'gy')
- residual: float32 [4, 24, 768, 512], P(None, None, 'gx', 'gy')
The draws below stay inside these ranges and needn't reach their ends.
All inputs are finite; a program needn't handle non-finite values.
Results may differ from the reference program's by a relative error of at most 0.0033.
Values sent between devices are 32-bit elements; how exact they have to be, the bound alone decides.
A program may use at most 128 MiB of HBM per device.

```python
import jax
import jax.numpy as jnp
from jax import lax

NRHS = 4
NZ = 24
NX = 768
NY = 512


def shard_levels(key, dims, shards, smallest, high):
    def one(position, parts):
        draws = jax.random.uniform(jax.random.fold_in(jax.random.fold_in(key, 6), position), (parts,), jnp.float32, smallest / len(shards), high / len(shards))
        return jnp.repeat(jnp.exp(draws), dims[position] // parts).reshape((-1,) + (1,) * (len(dims) - position - 1))

    level = one(*shards[0])
    for cut in shards[1:]:
        level = level * one(*cut)
    return level


def noise(own_key, shape, spread, limit, pieces=(), kind=jnp.bfloat16):
    result = spread * jax.random.normal(own_key, shape, jnp.float32)
    if pieces:
        result = result * shard_levels(own_key, shape, pieces, -0.22, 0.18)
    return jnp.clip(result, -limit, limit).astype(kind)


def setup_inputs(seed: int = 0) -> dict:
    key_list = jax.random.split(jax.random.key(seed), 5)
    return {
        "right_side": noise(key_list[0], (NRHS, NZ, NX, NY), 1.0, 8.0, ((2, 32), (3, 4)), jnp.float32),
        "start_field": noise(key_list[1], (NRHS, NZ, NX, NY), 0.5, 4.0, ((2, 32), (3, 4)), jnp.float32),
        "center": jnp.clip(0.5 + 2.5 * jax.random.uniform(key_list[2], (NZ, NX, NY), jnp.float32) ** shard_levels(key_list[2], (NZ, NX, NY), ((1, 32), (2, 4)), -0.2, 0.2), 0.5, 3.0),
        "weights": jnp.clip(0.4 + 1 * jax.random.uniform(key_list[3], (6, NZ, NX, NY), jnp.float32) ** shard_levels(key_list[3], (6, NZ, NX, NY), ((2, 32), (3, 4)), -0.2, 0.2), 0.4, 1.4),
    }


SHIFTS = (12.0, 2.0, 8.0, 5.0)
SCALE_DOWN = 5.0

def operate_padded(padded, center, weights):
    full = jnp.pad(padded, ((0, 0), (1, 1), (0, 0), (0, 0)))
    middle = full[:, 1:-1, 1:-1, 1:-1]
    beside = weights[0] * full[:, 1:-1, :-2, 1:-1] + weights[1] * full[:, 1:-1, 2:, 1:-1]
    beside = beside + weights[2] * full[:, 1:-1, 1:-1, :-2] + weights[3] * full[:, 1:-1, 1:-1, 2:]
    beside = beside + weights[4] * full[:, :-2, 1:-1, 1:-1] + weights[5] * full[:, 2:, 1:-1, 1:-1]
    return (6.0 + center) * middle - beside

def operate(field, center, weights):
    return operate_padded(jnp.pad(field, ((0, 0), (0, 0), (1, 1), (1, 1))), center, weights)

def reference(right_side, start_field, center, weights):
    first_res = right_side - operate(start_field, center, weights)
    basis = [first_res]
    for level in range(4):
        image = operate(basis[-1], center, weights)
        basis.append((image - SHIFTS[level] * basis[-1]) / SCALE_DOWN)

    def column(index):
        if index == 4:
            return first_res
        return SCALE_DOWN * basis[index + 1] + SHIFTS[index] * basis[index]
    blocks = [[None] * 5 for _ in range(5)]
    for first in range(5):
        left = column(first)
        for second in range(first, 5):
            right_part = left if second == first else column(second)
            block = jnp.einsum('rzxy,szxy->rs', left, right_part, precision=lax.Precision.HIGHEST)
            blocks[first][second] = block
            blocks[second][first] = block.T
    gram = jnp.block(blocks)
    lower_fac = jnp.linalg.cholesky(gram[:16, :16])
    middle_sol = jax.scipy.linalg.solve_triangular(lower_fac, gram[:16, 16:], lower=True)
    coeffs = jax.scipy.linalg.solve_triangular(lower_fac.T, middle_sol, lower=False)
    solution = start_field
    residual = first_res
    for level in range(4):
        part = coeffs[4 * level:4 * level + 4]
        solution = solution + jnp.einsum('szxy,sr->rzxy', basis[level], part, precision=lax.Precision.HIGHEST)
        residual = residual - jnp.einsum('szxy,sr->rzxy', column(level), part, precision=lax.Precision.HIGHEST)
    return (solution, residual)
```

```python
import functools

import jax
import jax.numpy as jnp
from jax import lax
from jax.experimental import pallas as pl
from jax.experimental.pallas import tpu as pltpu
from jax.sharding import PartitionSpec as P

SHIFTS = (12.0, 2.0, 8.0, 5.0)
SCALE_DOWN = 5.0
MESH = pl.DeviceIdType.MESH

R, NZ, BX, L = 4, 24, 24, 128
XT = BX // 8
FR = R * NZ * BX
WR = NZ * BX
PAD = 24
FS = FR + 2 * PAD


def pair_table():
    table, groups, at = {}, [], 0
    for level in range(4):
        for other in (level, 4) + tuple(range(level)):
            pairs = [
                (a, b)
                for a in range(R)
                for b in range(R)
                if other != level or b <= a
            ]
            for index, (a, b) in enumerate(pairs):
                table[(level, a, other, b)] = at + index
            groups.append((level, other, at, pairs))
            at += (len(pairs) + 7) // 8 * 8
    return table, groups, at


TABLE, GROUPS, USED = pair_table()
LANES = 256


def kernel(
    gx_size, gy_size, inner,
    b_hbm, x0_hbm, c_hbm, w_hbm,
    sol, res,
    F, W, B, C6, WM, WE, WX, HX, HY, XS, YS, HC, ACC, RED, RA, RB, CS,
    ld, sx, rx, sy, ry, sa, ra, sb, rb,
):
    gx = lax.axis_index("gx")
    gy = lax.axis_index("gy")
    outer = gx_size // inner
    base_x = (gx // inner) * inner
    in_x = gx - base_x

    loads = [
        pltpu.make_async_copy(x0_hbm, F.at[pl.ds(PAD, FR)], ld.at[0]),
        pltpu.make_async_copy(w_hbm, WM, ld.at[1]),
        pltpu.make_async_copy(c_hbm, C6, ld.at[2]),
        pltpu.make_async_copy(b_hbm, B, ld.at[3]),
    ]
    for copy in loads:
        copy.start()

    barrier = pltpu.get_barrier_semaphore()
    hello = []
    for step in (1, gx_size - 1):
        hello.append((lax.rem(gx + step, gx_size), gy))
    for step in (1, gy_size - 1):
        hello.append((gx, lax.rem(gy + step, gy_size)))
    inner_peers = [(base_x + lax.rem(in_x + i, inner), gy) for i in range(1, inner)]
    outer_peers = []
    for i in range(outer):
        for j in range(gy_size):
            if i or j:
                outer_peers.append(
                    (lax.rem(gx + i * inner, gx_size), lax.rem(gy + j, gy_size))
                )
    for peer in hello + inner_peers + outer_peers:
        pl.semaphore_signal(barrier, inc=1, device_id=peer, device_id_type=MESH)

    zero = jnp.zeros((8, L), jnp.float32)
    lane = lax.broadcasted_iota(jnp.int32, (8, L), 1)
    sub = lax.broadcasted_iota(jnp.int32, (8, L), 0)
    first_x, last_x = gx == 0, gx == gx_size - 1
    first_y, last_y = gy == 0, gy == gy_size - 1
    for f in range(5):
        for p in range(3):
            F[pl.ds(f * FS + 8 * p, 8), :] = zero
            F[pl.ds(f * FS + PAD + FR + 8 * p, 8), :] = zero

    def clear(ref, level, side):
        rows = ref.shape[2]
        for q in range(rows // 8):
            ref[level, side, pl.ds(8 * q, 8), :] = zero

    for cond, ref, side in (
        (first_x, HX, 0), (last_x, HX, 1), (first_y, HY, 0), (last_y, HY, 1),
    ):
        @pl.when(cond)
        def _(ref=ref, side=side):
            for level in range(5):
                clear(ref, level, side)

    def pack_masks(z):
        masks = []
        for half in range(2):
            j2 = 2 * (half * NZ + z)
            masks.append((((lane + 1 - j2) & (L - 1)) < 2, j2))
        return masks

    def tile_row(r, z, xt):
        return (r * NZ + z) * BX + 8 * xt

    def pack_tile(tile, r, xt, masks, acc):
        mask, j2 = masks[r % 2]
        at = (r // 2) * XT + xt
        acc[at] = jnp.where(mask, pltpu.roll(tile, j2, 1), acc[at])

    def store_packed(acc):
        for q in range(2 * XT):
            YS[pl.ds(8 * q, 8), :] = acc[q]

    def copies_x(level):
        return (
            (last_x, pltpu.make_async_remote_copy(
                src_ref=XS.at[level, 1], dst_ref=HX.at[level, 0],
                send_sem=sx.at[level, 1], recv_sem=rx.at[level, 0],
                device_id=(gx + 1, gy), device_id_type=MESH)),
            (first_x, pltpu.make_async_remote_copy(
                src_ref=XS.at[level, 0], dst_ref=HX.at[level, 1],
                send_sem=sx.at[level, 0], recv_sem=rx.at[level, 1],
                device_id=(gx - 1, gy), device_id_type=MESH)),
        )

    def copies_y(level):
        return (
            (last_y, pltpu.make_async_remote_copy(
                src_ref=YS, dst_ref=HY.at[level, 0],
                send_sem=sy.at[level, 1], recv_sem=ry.at[level, 0],
                device_id=(gx, gy + 1), device_id_type=MESH)),
            (first_y, pltpu.make_async_remote_copy(
                src_ref=YS, dst_ref=HY.at[level, 1],
                send_sem=sy.at[level, 0], recv_sem=ry.at[level, 1],
                device_id=(gx, gy - 1), device_id_type=MESH)),
        )

    def send(level, acc):
        store_packed(acc)
        for cond, copy in copies_y(level):
            @pl.when(jnp.logical_not(cond))
            def _(copy=copy):
                copy.start()
        for side, row in ((0, 0), (1, BX - 1)):
            for r in range(R):
                rows = F[pl.ds(level * FS + PAD + r * WR + row, NZ, stride=BX), :]
                XS[level, side, pl.ds(r * NZ, NZ), :] = rows
        for cond, copy in copies_x(level):
            @pl.when(jnp.logical_not(cond))
            def _(copy=copy):
                copy.start()

    def receive(level):
        for cond, (_, copy) in (
            (first_x, copies_x(level)[0]), (last_x, copies_x(level)[1]),
            (first_y, copies_y(level)[0]), (last_y, copies_y(level)[1]),
        ):
            @pl.when(jnp.logical_not(cond))
            def _(copy=copy):
                copy.wait_recv()
        for cond, copy in copies_x(level) + copies_y(level):
            @pl.when(jnp.logical_not(cond))
            def _(copy=copy):
                copy.wait_send()

    def bulk(level):
        base = level * FS + PAD
        out = max(level - 1, 0) * FR

        def body(z, carry):
            for xt in range(XT):
                wrow = pl.multiple_of(z * BX + 8 * xt, 8)
                w = [WM[pl.ds(k * WR + wrow, 8), :] for k in range(6)]
                c6 = C6[pl.ds(wrow, 8), :]
                for r in range(R):
                    row = pl.multiple_of(tile_row(r, z, xt), 8)
                    at = base + row
                    mid = F[pl.ds(at, 8), :]
                    beside = w[0] * F[pl.ds(at - 1, 8), :] + w[1] * F[pl.ds(at + 1, 8), :]
                    beside = beside + w[2] * pltpu.roll(mid, 1, 1) + w[3] * pltpu.roll(mid, L - 1, 1)
                    beside = beside + w[4] * F[pl.ds(at - BX, 8), :] + w[5] * F[pl.ds(at + BX, 8), :]
                    W[pl.ds(out + row, 8), :] = c6 * mid - beside
            return carry

        lax.fori_loop(0, NZ, body, 0)

    def correct(level):
        out = max(level - 1, 0) * FR
        for side, row in ((0, 0), (1, BX - 1)):
            for r in range(R):
                where = pl.ds(out + r * WR + row, NZ, stride=BX)
                W[where, :] = W[where, :] - (
                    WX[pl.ds(side * NZ, NZ), :] * HX[level, side, pl.ds(r * NZ, NZ), :]
                )
        even = (lane & 1) == 0
        for q in range(2 * XT):
            HC[pl.ds(8 * q, 8), :] = jnp.where(
                even,
                pltpu.roll(HY[level, 0, pl.ds(8 * q, 8), :], 1, 1),
                pltpu.roll(HY[level, 1, pl.ds(8 * q, 8), :], L - 1, 1),
            )

        def body(z, acc):
            acc = list(acc)
            masks = pack_masks(z)
            for xt in range(XT):
                edge = WE[pl.ds(pl.multiple_of(z * BX + 8 * xt, 8), 8), :]
                for r in range(R):
                    row = pl.multiple_of(tile_row(r, z, xt), 8)
                    halo = HC[pl.ds(8 * ((r // 2) * XT + xt), 8), :]
                    halo = pltpu.roll(halo, lax.rem(L - masks[r % 2][1], L), 1)
                    image = W[pl.ds(out + row, 8), :] - edge * halo
                    if level == 0:
                        following = B[pl.ds(row, 8), :] - image
                    else:
                        W[pl.ds(out + row, 8), :] = image
                        held = F[pl.ds(level * FS + PAD + row, 8), :]
                        following = (image - SHIFTS[level - 1] * held) * (1.0 / SCALE_DOWN)
                    if level < 4:
                        F[pl.ds((level + 1) * FS + PAD + row, 8), :] = following
                        pack_tile(following, r, xt, masks, acc)
            return tuple(acc)

        return lax.fori_loop(0, NZ, body, (zero,) * (2 * XT))

    def combine(a, b, d):
        mask = (sub & d) == 0
        return jnp.where(mask, a, b) + pltpu.roll(jnp.where(mask, b, a), d, 0)

    def gram(level):
        for lev, other, start, pairs in GROUPS:
            if lev != level:
                continue

            def rows_of(block, r, z, xt):
                row = pl.multiple_of(tile_row(r, z, xt), 8)
                if block == 4:
                    return F[pl.ds(FS + PAD + row, 8), :]
                return W[pl.ds(block * FR + row, 8), :]

            def body(z, acc):
                acc = list(acc)
                for xt in range(XT):
                    left = [rows_of(lev, r, z, xt) for r in range(R)]
                    right = left
                    if other != lev:
                        right = [rows_of(other, r, z, xt) for r in range(R)]
                    for index, (a, b) in enumerate(pairs):
                        acc[index] = acc[index] + left[a] * right[b]
                return tuple(acc)

            sums = list(lax.fori_loop(0, NZ, body, (zero,) * len(pairs)))
            sums += [zero] * (-len(sums) % 8)
            for q in range(0, len(sums), 8):
                part = sums[q : q + 8]
                for d in (1, 2, 4):
                    part = [combine(part[k], part[k + 1], d) for k in range(0, len(part), 2)]
                RED[pl.ds(start + q, 8), :] = part[0]

    loads[0].wait()

    def pack_body(z, acc):
        acc = list(acc)
        masks = pack_masks(z)
        for xt in range(XT):
            for r in range(R):
                row = pl.multiple_of(tile_row(r, z, xt), 8)
                pack_tile(F[pl.ds(PAD + row, 8), :], r, xt, masks, acc)
        return tuple(acc)

    acc = lax.fori_loop(0, NZ, pack_body, (zero,) * (2 * XT))
    pl.semaphore_wait(barrier, len(hello) + len(inner_peers) + len(outer_peers))
    send(0, acc)

    loads[1].wait()
    loads[2].wait()
    WX[pl.ds(0, NZ), :] = WM[pl.ds(0, NZ, stride=BX), :]
    WX[pl.ds(NZ, NZ), :] = WM[pl.ds(WR + BX - 1, NZ, stride=BX), :]

    def prepare(z, carry):
        for xt in range(XT):
            row = pl.multiple_of(z * BX + 8 * xt, 8)
            C6[pl.ds(row, 8), :] = C6[pl.ds(row, 8), :] + 6.0
            if xt == 0:
                WM[pl.ds(row, 8), :] = jnp.where(sub == 0, 0.0, WM[pl.ds(row, 8), :])
            if xt == XT - 1:
                at = WR + row
                WM[pl.ds(at, 8), :] = jnp.where(sub == 7, 0.0, WM[pl.ds(at, 8), :])
            low = WM[pl.ds(2 * WR + row, 8), :]
            high = WM[pl.ds(3 * WR + row, 8), :]
            WE[pl.ds(row, 8), :] = jnp.where(
                lane == 0, low, jnp.where(lane == L - 1, high, 0.0)
            )
            WM[pl.ds(2 * WR + row, 8), :] = jnp.where(lane == 0, 0.0, low)
            WM[pl.ds(3 * WR + row, 8), :] = jnp.where(lane == L - 1, 0.0, high)
        return carry

    lax.fori_loop(0, NZ, prepare, 0)
    for xt in range(XT):
        WM[pl.ds(4 * WR + 8 * xt, 8), :] = zero
        WM[pl.ds(5 * WR + (NZ - 1) * BX + 8 * xt, 8), :] = zero
    bulk(0)
    loads[3].wait()
    receive(0)
    acc = correct(0)
    for level in range(1, 5):
        send(level, acc)
        bulk(level)
        if level >= 2:
            gram(level - 2)
        receive(level)
        acc = correct(level)
    gram(3)

    for q in range(USED, LANES, 8):
        RED[pl.ds(q, 8), :] = zero
    total = lax.dot_general(
        jnp.ones((8, L), jnp.float32), RED[...], (((1,), (1,)), ((), ())),
        precision=lax.Precision.HIGHEST, preferred_element_type=jnp.float32,
    )

    def exchange(total, buffer, peers, send_sems, recv_sems):
        buffer[0] = total
        copies = []
        for k, peer in enumerate(peers):
            copy = pltpu.make_async_remote_copy(
                src_ref=buffer.at[0], dst_ref=buffer.at[k + 1],
                send_sem=send_sems.at[k], recv_sem=recv_sems.at[k],
                device_id=peer, device_id_type=MESH,
            )
            copy.start()
            copies.append(copy)
        for copy in copies:
            copy.wait_recv()
        parts = [buffer[k] for k in range(len(peers) + 1)]
        while len(parts) > 1:
            parts = [
                parts[k] + parts[k + 1] if k + 1 < len(parts) else parts[k]
                for k in range(0, len(parts), 2)
            ]
        for copy in copies:
            copy.wait_send()
        return parts[0]

    total = exchange(total, RA, inner_peers, sa, ra)
    total = exchange(total, RB, outer_peers, sb, rb)

    def entry(p):
        block = total[:, (p // L) * L : (p // L + 1) * L]
        return jnp.broadcast_to(block[:, p % L : p % L + 1], (8, L))

    order = 16
    A = {}
    for i in range(order):
        for j in range(i + 1):
            A[i, j] = entry(TABLE[(i // R, i % R, j // R, j % R)])
    rhs = []
    for i in range(order):
        column = [entry(TABLE[(i // R, i % R, 4, r)]) for r in range(R)]
        rhs.append(
            jnp.where(sub == 0, column[0],
                      jnp.where(sub == 1, column[1],
                                jnp.where(sub == 2, column[2], column[3])))
        )
    lower, inverse = {}, []
    for k in range(order):
        inv = 1.0 / A[k, k]
        inverse.append(inv)
        for i in range(k + 1, order):
            lower[i, k] = A[i, k] * inv
        for i in range(k + 1, order):
            for j in range(k + 1, i + 1):
                A[i, j] = A[i, j] - lower[i, k] * A[j, k]
            rhs[i] = rhs[i] - lower[i, k] * rhs[k]
    coeffs = [None] * order
    for k in range(order - 1, -1, -1):
        value = rhs[k] * inverse[k]
        for i in range(order - 1, k, -1):
            value = value - lower[i, k] * coeffs[i]
        coeffs[k] = value
        for r in range(R):
            CS[pl.ds((r * order + k) * 8, 8), :] = jnp.broadcast_to(value[r : r + 1], (8, L))

    for half in range(2):
        coef = [
            [CS[pl.ds(((2 * half + r) * order + k) * 8, 8), :] for k in range(order)]
            for r in range(2)
        ]

        def update(z, carry, half=half, coef=coef):
            for xt in range(XT):
                out = [pl.multiple_of(tile_row(2 * half + r, z, xt), 8) for r in range(2)]
                new_sol = [F[pl.ds(PAD + out[r], 8), :] for r in range(2)]
                new_res = [F[pl.ds(FS + PAD + out[r], 8), :] for r in range(2)]
                for k in range(order):
                    row = pl.multiple_of(tile_row(k % R, z, xt), 8)
                    basis = F[pl.ds((k // R + 1) * FS + PAD + row, 8), :]
                    image = W[pl.ds((k // R) * FR + row, 8), :]
                    for r in range(2):
                        new_sol[r] = new_sol[r] + coef[r][k] * basis
                        new_res[r] = new_res[r] - coef[r][k] * image
                for r in range(2):
                    sol[pl.ds(out[r], 8), :] = new_sol[r]
                    res[pl.ds(out[r], 8), :] = new_res[r]
            return carry

        lax.fori_loop(0, NZ, update, 0)


def on_device(gx_size, gy_size, right_side, start_field, center, weights):
    inner = min(8, gx_size // 2)
    outer = gx_size // inner
    dma = pltpu.SemaphoreType.DMA
    f32 = jnp.float32
    flat = lambda a: a.reshape(-1, L)
    out = pl.pallas_call(
        functools.partial(kernel, gx_size, gy_size, inner),
        out_shape=[jax.ShapeDtypeStruct((FR, L), f32)] * 2,
        in_specs=[pl.BlockSpec(memory_space=pltpu.HBM)] * 4,
        out_specs=[pl.BlockSpec(memory_space=pltpu.VMEM)] * 2,
        scratch_shapes=[
            pltpu.VMEM((5 * FS, L), f32),
            pltpu.VMEM((4 * FR, L), f32),
            pltpu.VMEM((FR, L), f32),
            pltpu.VMEM((WR, L), f32),
            pltpu.VMEM((6 * WR, L), f32),
            pltpu.VMEM((WR, L), f32),
            pltpu.VMEM((2 * NZ, L), f32),
            pltpu.VMEM((5, 2, R * NZ, L), f32),
            pltpu.VMEM((5, 2, 2 * BX, L), f32),
            pltpu.VMEM((5, 2, R * NZ, L), f32),
            pltpu.VMEM((2 * BX, L), f32),
            pltpu.VMEM((2 * BX, L), f32),
            pltpu.VMEM((8, L), f32),
            pltpu.VMEM((LANES, L), f32),
            pltpu.VMEM((inner, 8, LANES), f32),
            pltpu.VMEM((outer * gy_size, 8, LANES), f32),
            pltpu.VMEM((64 * 8, L), f32),
            dma((4,)),
            dma((5, 2)), dma((5, 2)), dma((5, 2)), dma((5, 2)),
            dma((inner,)), dma((inner,)),
            dma((outer * gy_size,)), dma((outer * gy_size,)),
        ],
        compiler_params=pltpu.CompilerParams(
            collective_id=0, has_side_effects=True, vmem_limit_bytes=48 * 1024 * 1024,
        ),
    )(flat(right_side), flat(start_field), flat(center), flat(weights))
    return tuple(o.reshape(R, NZ, BX, L) for o in out)


def solution(mesh):
    gx_size, gy_size = mesh.shape["gx"], mesh.shape["gy"]
    return jax.shard_map(
        functools.partial(on_device, gx_size, gy_size),
        mesh=mesh,
        in_specs=(
            P(None, None, "gx", "gy"),
            P(None, None, "gx", "gy"),
            P(None, "gx", "gy"),
            P(None, None, "gx", "gy"),
        ),
        out_specs=(P(None, None, "gx", "gy"), P(None, None, "gx", "gy")),
        check_vma=False,
    )
```

```python
import functools

import jax
import jax.numpy as jnp
from jax import lax
from jax.experimental import pallas as pl
from jax.experimental.pallas import tpu as pltpu
from jax.sharding import PartitionSpec as P

SHIFTS = (12.0, 2.0, 8.0, 5.0)
SCALE_DOWN = 5.0
MESH = pl.DeviceIdType.MESH

R, NZ, BX, L = 4, 24, 24, 128
XT = BX // 8
FR = R * NZ * BX
WR = NZ * BX
PAD = 24
FS = FR + 2 * PAD
HALF = NZ // 2
GROUP = 4
STEPS = NZ // GROUP


def pair_table():
    table, groups, at = {}, [], 0
    for level in range(4):
        for other in (level, 4) + tuple(range(level)):
            pairs = [
                (a, b)
                for a in range(R)
                for b in range(R)
                if other != level or b <= a
            ]
            for index, (a, b) in enumerate(pairs):
                table[(level, a, other, b)] = at + index
            groups.append((level, other, at, pairs))
            at += (len(pairs) + 7) // 8 * 8
    return table, groups, at


TABLE, GROUPS, USED = pair_table()
LANES = 256


def kernel(
    gx_size, gy_size, inner,
    b_hbm, x0_hbm, c_hbm, w_hbm,
    F, W, CS,
    B, C6, WM, WE, WX, HX, HY, XS, YS, HC, RING, RED, RA, RB,
    ld, sx, rx, sy, ry, sa, ra, sb, rb,
):
    gx = lax.axis_index("gx")
    gy = lax.axis_index("gy")
    outer = gx_size // inner
    base_x = (gx // inner) * inner
    in_x = gx - base_x

    loads = [[], [], [], []]
    for group, (source, ref, offset, parts) in enumerate((
        (x0_hbm, F, PAD, R), (w_hbm, WM, 0, 6), (c_hbm, C6, 0, 1), (b_hbm, B, 0, R),
    )):
        rows = source.shape[0] // parts
        for part in range(parts):
            copy = pltpu.make_async_copy(
                source.at[pl.ds(part * rows, rows)],
                ref.at[pl.ds(offset + part * rows, rows)],
                ld.at[group, part],
            )
            copy.start()
            loads[group].append(copy)

    barrier = pltpu.get_barrier_semaphore()
    hello = []
    for step in (1, gx_size - 1):
        hello.append((lax.rem(gx + step, gx_size), gy))
    for step in (1, gy_size - 1):
        hello.append((gx, lax.rem(gy + step, gy_size)))
    inner_peers = [(base_x + lax.rem(in_x + i, inner), gy) for i in range(1, inner)]
    outer_peers = []
    for i in range(outer):
        for j in range(gy_size):
            if i or j:
                outer_peers.append(
                    (lax.rem(gx + i * inner, gx_size), lax.rem(gy + j, gy_size))
                )
    for peer in hello + inner_peers + outer_peers:
        pl.semaphore_signal(barrier, inc=1, device_id=peer, device_id_type=MESH)

    zero = jnp.zeros((8, L), jnp.float32)
    lane = lax.broadcasted_iota(jnp.int32, (8, L), 1)
    sub = lax.broadcasted_iota(jnp.int32, (8, L), 0)
    first_x, last_x = gx == 0, gx == gx_size - 1
    first_y, last_y = gy == 0, gy == gy_size - 1
    for f in range(5):
        for p in range(3):
            F[pl.ds(f * FS + 8 * p, 8), :] = zero
            F[pl.ds(f * FS + PAD + FR + 8 * p, 8), :] = zero

    for cond, ref, side in (
        (first_x, HX, 0), (last_x, HX, 1), (first_y, HY, 0), (last_y, HY, 1),
    ):
        @pl.when(cond)
        def _(ref=ref, side=side):
            for level in range(5):
                for half in range(2):
                    for q in range(ref.shape[3] // 8):
                        ref[level, half, side, pl.ds(8 * q, 8), :] = zero

    tiles = [(xt, r) for xt in range(XT) for r in range(R)]

    def tile_row(r, z, xt):
        return (r * NZ + z) * BX + 8 * xt

    def aligned(row):
        return row if isinstance(row, int) else pl.multiple_of(row, 8)

    def pack_lane(r, zh):
        return 2 * (r * HALF + zh)

    def pack_tile(tile, r, zh, acc):
        j2 = pack_lane(r, zh)
        mask = ((lane + (1 - j2)) & (L - 1)) < 2
        return jnp.where(mask, pltpu.roll(tile, j2, 1), acc)

    def copies(level, half):
        result = []
        for missing, lands, takes, gap, row in (
            (last_x, 0, 1, (gx + 1, gy), XS), (first_x, 1, 0, (gx - 1, gy), XS),
            (last_y, 0, None, (gx, gy + 1), YS), (first_y, 1, None, (gx, gy - 1), YS),
        ):
            along_x = row is XS
            source = XS.at[level, half, takes] if along_x else YS.at[level, half]
            target = (HX if along_x else HY).at[level, half, lands]
            out_sem, in_sem = (sx, rx) if along_x else (sy, ry)
            result.append((missing, pltpu.make_async_remote_copy(
                src_ref=source, dst_ref=target,
                send_sem=out_sem.at[level, half, lands], recv_sem=in_sem.at[level, half, lands],
                device_id=gap, device_id_type=MESH)))
        return result

    def send(level, half, acc):
        for xt in range(XT):
            YS[level, half, pl.ds(8 * xt, 8), :] = acc[xt]
        for missing, copy in copies(level, half):
            @pl.when(jnp.logical_not(missing))
            def _(copy=copy):
                copy.start()

    def receive(level, half):
        for missing, (_, copy) in zip(
            (first_x, last_x, first_y, last_y), copies(level, half)
        ):
            @pl.when(jnp.logical_not(missing))
            def _(copy=copy):
                copy.wait_recv()

    def sent(level):
        for half in range(2):
            for missing, copy in copies(level, half):
                @pl.when(jnp.logical_not(missing))
                def _(copy=copy):
                    copy.wait_send()

    def bulk(level):
        base = level * FS + PAD
        out = max(level - 1, 0) * FR
        slot = 2 * GROUP * R * XT * 8

        def keep_rolls(z0, at):
            kept = []
            for k in range(GROUP):
                for index, (xt, r) in enumerate(tiles):
                    mid = F[pl.ds(aligned(base + tile_row(r, z0 + k, xt)), 8), :]
                    where = at + 16 * (k * R * XT + index)
                    kept.append((where, pltpu.roll(mid, 1, 1)))
                    kept.append((where + 8, pltpu.roll(mid, L - 1, 1)))
            return kept

        for at, value in keep_rolls(0, 0):
            RING[pl.ds(at, 8), :] = value

        def body(step, carry):
            now = pl.multiple_of(lax.rem(step, 2) * slot, 8)
            later = pl.multiple_of(slot - now, 8)
            kept = keep_rolls(jnp.minimum(step + 1, STEPS - 1) * GROUP, later)
            stores = []
            for k in range(GROUP):
                z = step * GROUP + k
                for xt in range(XT):
                    wrow = pl.multiple_of(z * BX + 8 * xt, 8)
                    w = [WM[pl.ds(i * WR + wrow, 8), :] for i in range(6)]
                    c6 = C6[pl.ds(wrow, 8), :]
                    for r in range(R):
                        ring = now + 16 * ((k * XT + xt) * R + r)
                        row = pl.multiple_of(tile_row(r, z, xt), 8)
                        at = base + row
                        low = RING[pl.ds(ring, 8), :]
                        high = RING[pl.ds(ring + 8, 8), :]
                        beside = w[0] * F[pl.ds(at - 1, 8), :] + w[1] * F[pl.ds(at + 1, 8), :]
                        beside = beside + (w[2] * low + w[3] * high)
                        beside = beside + (
                            w[4] * F[pl.ds(at - BX, 8), :] + w[5] * F[pl.ds(at + BX, 8), :]
                        )
                        stores.append((out + row, c6 * F[pl.ds(at, 8), :] - beside))
            for at, value in stores:
                W[pl.ds(at, 8), :] = value
            for at, value in kept:
                RING[pl.ds(at, 8), :] = value
            return carry

        lax.fori_loop(0, STEPS, body, 0)

    def correct(level, half):
        out = max(level - 1, 0) * FR
        even = (lane & 1) == 0
        for xt in range(XT):
            HC[pl.ds(8 * xt, 8), :] = jnp.where(
                even,
                pltpu.roll(HY[level, half, 0, pl.ds(8 * xt, 8), :], 1, 1),
                pltpu.roll(HY[level, half, 1, pl.ds(8 * xt, 8), :], L - 1, 1),
            )
        slot = GROUP * R * XT * 8
        ahead = (level + 1) * FS + PAD
        steps = HALF // GROUP

        def keep_halos(step, at):
            kept = []
            for k in range(GROUP):
                for index, (xt, r) in enumerate(tiles):
                    back = lax.rem(2 * L - pack_lane(r, step * GROUP + k), L)
                    halo = pltpu.roll(HC[pl.ds(8 * xt, 8), :], back, 1)
                    kept.append((at + 8 * (k * R * XT + index), halo))
            return kept

        def pack_planes(step, acc):
            for k in range(GROUP):
                zh = step * GROUP + k
                for xt, r in tiles:
                    row = aligned(tile_row(r, half * HALF + zh, xt))
                    acc[xt] = pack_tile(F[pl.ds(ahead + row, 8), :], r, zh, acc[xt])

        for at, value in keep_halos(0, 0):
            RING[pl.ds(at, 8), :] = value

        def body(step, acc):
            acc = list(acc)
            now = pl.multiple_of(lax.rem(step, 2) * slot, 8)
            later = pl.multiple_of(slot - now, 8)
            kept = keep_halos(jnp.minimum(step + 1, steps - 1), later)
            if level < 4:
                pack_planes(jnp.maximum(step - 1, 0), acc)
            stores, nexts, rows = [], [], []
            for k in range(GROUP):
                zh = step * GROUP + k
                z = half * HALF + zh
                for xt in range(XT):
                    edge = WE[pl.ds(pl.multiple_of(z * BX + 8 * xt, 8), 8), :]
                    for r in range(R):
                        row = pl.multiple_of(tile_row(r, z, xt), 8)
                        halo = RING[pl.ds(now + 8 * ((k * XT + xt) * R + r), 8), :]
                        image = W[pl.ds(out + row, 8), :] - edge * halo
                        for side, where in ((0, 0), (1, XT - 1)):
                            if xt == where:
                                edge_x = WX[pl.ds(pl.multiple_of((side * NZ + z) * 8, 8), 8), :]
                                halo_x = HX[level, half, side, pl.ds(r * HALF + zh, 1), :]
                                image = image - edge_x * jnp.broadcast_to(halo_x, (8, L))
                        if level == 0:
                            following = B[pl.ds(row, 8), :] - image
                        else:
                            stores.append((out + row, image))
                            held = F[pl.ds(level * FS + PAD + row, 8), :]
                            following = image * (1.0 / SCALE_DOWN) - held * (
                                SHIFTS[level - 1] / SCALE_DOWN
                            )
                        if level < 4:
                            nexts.append((ahead + row, following))
                            for side, where, take in ((0, 0, 0), (1, XT - 1, 7)):
                                if xt == where:
                                    rows.append((side, r * HALF + zh, following[take : take + 1]))
            for at, value in stores:
                W[pl.ds(at, 8), :] = value
            for at, value in nexts:
                F[pl.ds(at, 8), :] = value
            for side, at, value in rows:
                XS[level + 1, half, side, pl.ds(at, 1), :] = value
            for at, value in kept:
                RING[pl.ds(at, 8), :] = value
            return tuple(acc)

        acc = list(lax.fori_loop(0, steps, body, (zero,) * XT))
        if level < 4:
            pack_planes(steps - 1, acc)
        return acc

    def combine(a, b, d):
        mask = (sub & d) == 0
        return jnp.where(mask, a, b) + pltpu.roll(jnp.where(mask, b, a), d, 0)

    def gram(level):
        for lev, other, start, pairs in GROUPS:
            if lev != level:
                continue

            def rows_of(block, r, z, xt):
                row = pl.multiple_of(tile_row(r, z, xt), 8)
                if block == 4:
                    return F[pl.ds(FS + PAD + row, 8), :]
                return W[pl.ds(block * FR + row, 8), :]

            def body(step, acc):
                acc = list(acc)
                for z, xt in [(2 * step + k, xt) for k in range(2) for xt in range(XT)]:
                    left = [rows_of(lev, r, z, xt) for r in range(R)]
                    right = left
                    if other != lev:
                        right = [rows_of(other, r, z, xt) for r in range(R)]
                    for index, (a, b) in enumerate(pairs):
                        acc[index] = acc[index] + left[a] * right[b]
                return tuple(acc)

            sums = list(lax.fori_loop(0, NZ // 2, body, (zero,) * len(pairs)))
            sums += [zero] * (-len(sums) % 8)
            for q in range(0, len(sums), 8):
                part = sums[q : q + 8]
                for d in (1, 2, 4):
                    part = [combine(part[k], part[k + 1], d) for k in range(0, len(part), 2)]
                RED[pl.ds(start + q, 8), :] = part[0]

    for copy in loads[0]:
        copy.wait()

    packed = []
    for half in range(2):
        def pack_body(step, acc, half=half):
            acc = list(acc)
            for k in range(GROUP):
                zh = step * GROUP + k
                for xt, r in tiles:
                    row = pl.multiple_of(PAD + tile_row(r, half * HALF + zh, xt), 8)
                    tile = F[pl.ds(row, 8), :]
                    acc[xt] = pack_tile(tile, r, zh, acc[xt])
                    for side, where, take in ((0, 0, 0), (1, XT - 1, 7)):
                        if xt == where:
                            XS[0, half, side, pl.ds(r * HALF + zh, 1), :] = tile[take : take + 1]
            return tuple(acc)

        packed.append(lax.fori_loop(0, HALF // GROUP, pack_body, (zero,) * XT))
    pl.semaphore_wait(barrier, len(hello) + len(inner_peers) + len(outer_peers))
    for half in range(2):
        send(0, half, packed[half])

    for copy in loads[1] + loads[2]:
        copy.wait()

    def prepare(z, carry):
        stores = []
        for xt in range(XT):
            row = pl.multiple_of(z * BX + 8 * xt, 8)
            stores.append((C6, row, C6[pl.ds(row, 8), :] + 6.0))
            for side, where, inside in ((0, 0, sub != 0), (1, XT - 1, sub != 7)):
                if xt == where:
                    w = WM[pl.ds(side * WR + row, 8), :]
                    stores.append((WM, side * WR + row, jnp.where(inside, w, 0.0)))
                    at = pl.multiple_of((side * NZ + z) * 8, 8)
                    stores.append((WX, at, jnp.where(inside, 0.0, w)))
            low = WM[pl.ds(2 * WR + row, 8), :]
            high = WM[pl.ds(3 * WR + row, 8), :]
            edge = jnp.where(lane == 0, low, jnp.where(lane == L - 1, high, 0.0))
            stores.append((WE, row, edge))
            stores.append((WM, 2 * WR + row, jnp.where(lane == 0, 0.0, low)))
            stores.append((WM, 3 * WR + row, jnp.where(lane == L - 1, 0.0, high)))
        for ref, at, value in stores:
            ref[pl.ds(at, 8), :] = value
        return carry

    lax.fori_loop(0, NZ, prepare, 0)
    for xt in range(XT):
        WM[pl.ds(4 * WR + 8 * xt, 8), :] = zero
        WM[pl.ds(5 * WR + (NZ - 1) * BX + 8 * xt, 8), :] = zero
    bulk(0)
    for copy in loads[3]:
        copy.wait()
    for level in range(5):
        for half in range(2):
            receive(level, half)
            acc = correct(level, half)
            if level < 4:
                send(level + 1, half, acc)
        if level < 4:
            bulk(level + 1)
            if level >= 1:
                gram(level - 1)
        sent(level)
    gram(3)

    for q in range(USED, LANES, 8):
        RED[pl.ds(q, 8), :] = zero
    total = lax.dot_general(
        jnp.ones((8, L), jnp.float32), RED[...], (((1,), (1,)), ((), ())),
        precision=lax.Precision.HIGHEST, preferred_element_type=jnp.float32,
    )

    def exchange(total, buffer, peers, send_sems, recv_sems):
        buffer[0] = total
        copies = []
        for k, peer in enumerate(peers):
            copy = pltpu.make_async_remote_copy(
                src_ref=buffer.at[0], dst_ref=buffer.at[k + 1],
                send_sem=send_sems.at[k], recv_sem=recv_sems.at[k],
                device_id=peer, device_id_type=MESH,
            )
            copy.start()
            copies.append(copy)
        for copy in copies:
            copy.wait_recv()
        parts = [buffer[k] for k in range(len(peers) + 1)]
        while len(parts) > 1:
            parts = [
                parts[k] + parts[k + 1] if k + 1 < len(parts) else parts[k]
                for k in range(0, len(parts), 2)
            ]
        for copy in copies:
            copy.wait_send()
        return parts[0]

    total = exchange(total, RA, inner_peers, sa, ra)
    total = exchange(total, RB, outer_peers, sb, rb)

    def entry(p):
        block = total[:, (p // L) * L : (p // L + 1) * L]
        return jnp.broadcast_to(block[:, p % L : p % L + 1], (8, L))

    order = 16
    A = {}
    for i in range(order):
        for j in range(i + 1):
            A[i, j] = entry(TABLE[(i // R, i % R, j // R, j % R)])
    rhs = []
    for i in range(order):
        column = [entry(TABLE[(i // R, i % R, 4, r)]) for r in range(R)]
        rhs.append(
            jnp.where(sub == 0, column[0],
                      jnp.where(sub == 1, column[1],
                                jnp.where(sub == 2, column[2], column[3])))
        )
    lower, inverse = {}, []
    for k in range(order):
        inv = 1.0 / A[k, k]
        inverse.append(inv)
        for i in range(k + 1, order):
            lower[i, k] = A[i, k] * inv
        for i in range(k + 1, order):
            for j in range(k + 1, i + 1):
                A[i, j] = A[i, j] - lower[i, k] * A[j, k]
            rhs[i] = rhs[i] - lower[i, k] * rhs[k]
    coeffs = [None] * order
    for k in range(order - 1, -1, -1):
        value = rhs[k] * inverse[k]
        for i in range(order - 1, k, -1):
            value = value - lower[i, k] * coeffs[i]
        coeffs[k] = value
        for r in range(R):
            CS[pl.ds((r * order + k) * 8, 8), :] = jnp.broadcast_to(value[r : r + 1], (8, L))


def update(F, W, CS, x0, sol, res):
    step = pl.program_id(0)
    planes = NZ // UPDATE_STEPS

    def body(k, carry):
        z = step * planes + k
        stores = []
        for r in range(R):
            for xt in range(XT):
                row = pl.multiple_of((r * NZ + z) * BX + 8 * xt, 8)
                stores.append([x0[r, k, pl.ds(8 * xt, 8), :], F[pl.ds(FS + PAD + row, 8), :]])
        for i in range(16):
            coef = [CS[pl.ds((r * 16 + i) * 8, 8), :] for r in range(R)]
            for xt in range(XT):
                row = pl.multiple_of(((i % R) * NZ + z) * BX + 8 * xt, 8)
                basis = F[pl.ds((i // R + 1) * FS + PAD + row, 8), :]
                image = W[pl.ds((i // R) * FR + row, 8), :]
                for r in range(R):
                    both = stores[r * XT + xt]
                    both[0] = both[0] + coef[r] * basis
                    both[1] = both[1] - coef[r] * image
        for r in range(R):
            for xt in range(XT):
                sol[r, k, pl.ds(8 * xt, 8), :] = stores[r * XT + xt][0]
                res[r, k, pl.ds(8 * xt, 8), :] = stores[r * XT + xt][1]
        return carry

    lax.fori_loop(0, planes, body, 0)


UPDATE_STEPS = 4


def on_device(gx_size, gy_size, right_side, start_field, center, weights):
    inner = min(8, gx_size // 2)
    outer = gx_size // inner
    dma = pltpu.SemaphoreType.DMA
    f32 = jnp.float32
    flat = lambda a: a.reshape(-1, L)
    held = pltpu.MemorySpace.VMEM
    shape = lambda *dims: jax.ShapeDtypeStruct(dims, f32)
    in_hbm = lambda a: pltpu.with_memory_space_constraint(flat(a), pltpu.HBM)
    fields, images, coeffs = pl.pallas_call(
        functools.partial(kernel, gx_size, gy_size, inner),
        out_shape=[shape(5 * FS, L), shape(4 * FR, L), shape(64 * 8, L)],
        in_specs=[pl.BlockSpec(memory_space=pltpu.HBM)] * 4,
        out_specs=[pl.BlockSpec(memory_space=held)] * 3,
        scratch_shapes=[
            pltpu.VMEM((FR, L), f32),
            pltpu.VMEM((WR, L), f32),
            pltpu.VMEM((6 * WR, L), f32),
            pltpu.VMEM((WR, L), f32),
            pltpu.VMEM((2 * NZ * 8, L), f32),
            pltpu.VMEM((5, 2, 2, R * HALF, L), f32),
            pltpu.VMEM((5, 2, 2, BX, L), f32),
            pltpu.VMEM((5, 2, 2, R * HALF, L), f32),
            pltpu.VMEM((5, 2, BX, L), f32),
            pltpu.VMEM((BX, L), f32),
            pltpu.VMEM((2 * 2 * GROUP * R * XT * 8, L), f32),
            pltpu.VMEM((LANES, L), f32),
            pltpu.VMEM((inner, 8, LANES), f32),
            pltpu.VMEM((outer * gy_size, 8, LANES), f32),
            dma((4, 6)),
            dma((5, 2, 2)), dma((5, 2, 2)), dma((5, 2, 2)), dma((5, 2, 2)),
            dma((inner,)), dma((inner,)),
            dma((outer * gy_size,)), dma((outer * gy_size,)),
        ],
        compiler_params=pltpu.CompilerParams(
            collective_id=0, has_side_effects=True, vmem_limit_bytes=32 * 1024 * 1024,
        ),
    )(in_hbm(right_side), in_hbm(start_field), in_hbm(center), in_hbm(weights))
    block = pl.BlockSpec((R, NZ // UPDATE_STEPS, BX, L), lambda i: (0, i, 0, 0))
    return pl.pallas_call(
        update,
        grid=(UPDATE_STEPS,),
        out_shape=[shape(R, NZ, BX, L)] * 2,
        in_specs=[pl.BlockSpec(memory_space=held)] * 3 + [block],
        out_specs=[block, block],
        compiler_params=pltpu.CompilerParams(vmem_limit_bytes=24 * 1024 * 1024),
    )(fields, images, coeffs, pltpu.with_memory_space_constraint(start_field, pltpu.HBM))


def solution(mesh):
    gx_size, gy_size = mesh.shape["gx"], mesh.shape["gy"]
    return jax.shard_map(
        functools.partial(on_device, gx_size, gy_size),
        mesh=mesh,
        in_specs=(
            P(None, None, "gx", "gy"),
            P(None, None, "gx", "gy"),
            P(None, "gx", "gy"),
            P(None, None, "gx", "gy"),
        ),
        out_specs=(P(None, None, "gx", "gy"), P(None, None, "gx", "gy")),
        check_vma=False,
    )
```

```python
import functools

import jax
import jax.numpy as jnp
from jax import lax
from jax.experimental import pallas as pl
from jax.experimental.pallas import tpu as pltpu
from jax.sharding import PartitionSpec as P

SHIFTS = (12.0, 2.0, 8.0, 5.0)
SCALE_DOWN = 5.0
MESH = pl.DeviceIdType.MESH

R, NZ, BX, L = 4, 24, 24, 128
XT = BX // 8
FR = R * NZ * BX
WR = NZ * BX
PAD = 24
FS = FR + 2 * PAD
HALF = NZ // 2
GROUP = 4
STEPS = NZ // GROUP


def pair_table():
    table, groups, at = {}, [], 0
    for level in range(4):
        for other in (level, 4) + tuple(range(level)):
            pairs = [
                (a, b)
                for a in range(R)
                for b in range(R)
                if other != level or b <= a
            ]
            for index, (a, b) in enumerate(pairs):
                table[(level, a, other, b)] = at + index
            groups.append((level, other, at, pairs))
            at += (len(pairs) + 7) // 8 * 8
    return table, groups, at


TABLE, GROUPS, USED = pair_table()
LANES = 256


def kernel(
    gx_size, gy_size, inner,
    b_hbm, x0_hbm, c_hbm, w_hbm,
    F, W, CS,
    B, C6, WM, WE, WX, HX, HY, XS, YS, RING, ACC, RED, RA, RB,
    ld, sx, rx, sy, ry, sa, ra, sb, rb,
):
    gx = lax.axis_index("gx")
    gy = lax.axis_index("gy")
    outer = gx_size // inner
    base_x = (gx // inner) * inner
    in_x = gx - base_x

    loads = [[], [], [], []]
    for group, (source, ref, offset, parts) in enumerate((
        (x0_hbm, F, PAD, R), (w_hbm, WM, 0, 6), (c_hbm, C6, 0, 1), (b_hbm, B, 0, R),
    )):
        rows = source.shape[0] // parts
        for part in range(parts):
            copy = pltpu.make_async_copy(
                source.at[pl.ds(part * rows, rows)],
                ref.at[pl.ds(offset + part * rows, rows)],
                ld.at[group, part],
            )
            loads[group].append(copy)
    for copy in loads[0] + loads[2] + loads[1]:
        copy.start()

    barrier = pltpu.get_barrier_semaphore()
    hello = []
    for step in (1, gx_size - 1):
        hello.append((lax.rem(gx + step, gx_size), gy))
    for step in (1, gy_size - 1):
        hello.append((gx, lax.rem(gy + step, gy_size)))
    inner_peers = [(base_x + lax.rem(in_x + i, inner), gy) for i in range(1, inner)]
    outer_peers = []
    for i in range(outer):
        for j in range(gy_size):
            if i or j:
                outer_peers.append(
                    (lax.rem(gx + i * inner, gx_size), lax.rem(gy + j, gy_size))
                )
    for peer in hello + inner_peers + outer_peers:
        pl.semaphore_signal(barrier, inc=1, device_id=peer, device_id_type=MESH)

    zero = jnp.zeros((8, L), jnp.float32)
    lane = lax.broadcasted_iota(jnp.int32, (8, L), 1)
    sub = lax.broadcasted_iota(jnp.int32, (8, L), 0)
    first_x, last_x = gx == 0, gx == gx_size - 1
    first_y, last_y = gy == 0, gy == gy_size - 1
    for f in range(5):
        for p in range(3):
            F[pl.ds(f * FS + 8 * p, 8), :] = zero
            F[pl.ds(f * FS + PAD + FR + 8 * p, 8), :] = zero

    for cond, ref, side in (
        (first_x, HX, 0), (last_x, HX, 1), (first_y, HY, 0), (last_y, HY, 1),
    ):
        @pl.when(cond)
        def _(ref=ref, side=side):
            for level in range(5):
                for half in range(2):
                    for q in range(ref.shape[3] // 8):
                        ref[level, half, side, pl.ds(8 * q, 8), :] = zero

    tiles = [(xt, r) for xt in range(XT) for r in range(R)]

    def tile_row(r, z, xt):
        return (r * NZ + z) * BX + 8 * xt

    def aligned(row):
        return row if isinstance(row, int) else pl.multiple_of(row, 8)

    def pack_lane(r, zh):
        return 2 * (r * HALF + zh)

    def pack_tile(tile, r, zh, acc):
        j2 = pack_lane(r, zh)
        mask = ((lane + (1 - j2)) & (L - 1)) < 2
        return jnp.where(mask, pltpu.roll(tile, j2, 1), acc)

    def copies(level, half):
        result = []
        for missing, lands, takes, gap, row in (
            (last_x, 0, 1, (gx + 1, gy), XS), (first_x, 1, 0, (gx - 1, gy), XS),
            (last_y, 0, None, (gx, gy + 1), YS), (first_y, 1, None, (gx, gy - 1), YS),
        ):
            along_x = row is XS
            source = XS.at[level, half, takes] if along_x else YS.at[level, half]
            target = (HX if along_x else HY).at[level, half, lands]
            out_sem, in_sem = (sx, rx) if along_x else (sy, ry)
            result.append((missing, pltpu.make_async_remote_copy(
                src_ref=source, dst_ref=target,
                send_sem=out_sem.at[level, half, lands], recv_sem=in_sem.at[level, half, lands],
                device_id=gap, device_id_type=MESH)))
        return result

    def send(level, half, acc):
        for xt in range(XT):
            YS[level, half, pl.ds(8 * xt, 8), :] = acc[xt]
        for missing, copy in copies(level, half):
            @pl.when(jnp.logical_not(missing))
            def _(copy=copy):
                copy.start()

    def receive(level, half):
        for missing, (_, copy) in zip(
            (first_x, last_x, first_y, last_y), copies(level, half)
        ):
            @pl.when(jnp.logical_not(missing))
            def _(copy=copy):
                copy.wait_recv()

    def sent(level):
        for half in range(2):
            for missing, copy in copies(level, half):
                @pl.when(jnp.logical_not(missing))
                def _(copy=copy):
                    copy.wait_send()

    slot = 2 * GROUP * R * XT * 8

    def keep_rolls(level, z0, at):
            base = level * FS + PAD
            kept = []
            for k in range(GROUP):
                for index, (xt, r) in enumerate(tiles):
                    mid = F[pl.ds(aligned(base + tile_row(r, z0 + k, xt)), 8), :]
                    where = at + 16 * (k * R * XT + index)
                    kept.append((where, pltpu.roll(mid, 1, 1)))
                    kept.append((where + 8, pltpu.roll(mid, L - 1, 1)))
            return kept

    def first_rolls(level):
        for at, value in keep_rolls(level, 0, 0):
            RING[pl.ds(at, 8), :] = value

    def rows_of(block, r, z, xt):
        row = aligned(tile_row(r, z, xt))
        if block == 4:
            return F[pl.ds(FS + PAD + row, 8), :]
        return W[pl.ds(block * FR + row, 8), :]

    def products(lev, other, pairs, places, acc):
        for z, xt in places:
            left = [rows_of(lev, r, z, xt) for r in range(R)]
            right = left if other == lev else [rows_of(other, r, z, xt) for r in range(R)]
            for index, (a, b) in enumerate(pairs):
                acc[index] = acc[index] + left[a] * right[b]

    def fold(sums, start):
        sums = sums + [zero] * (-len(sums) % 8)
        for q in range(0, len(sums), 8):
            part = sums[q : q + 8]
            for d in (1, 2, 4):
                part = [combine(part[k], part[k + 1], d) for k in range(0, len(part), 2)]
            RED[pl.ds(start + q, 8), :] = part[0]

    def bulk(level, gram_level=None):
        base = level * FS + PAD
        out = max(level - 1, 0) * FR
        groups = [g for g in GROUPS if g[0] == gram_level]
        for _, _, start, pairs in groups:
            for index in range(len(pairs)):
                ACC[pl.ds(8 * (start + index), 8), :] = zero

        def body(step, carry):
            now = pl.multiple_of(lax.rem(step, 2) * slot, 8)
            later = pl.multiple_of(slot - now, 8)
            kept = keep_rolls(level, jnp.minimum(step + 1, STEPS - 1) * GROUP, later)
            stores = []
            for k in range(GROUP):
                z = step * GROUP + k
                for xt in range(XT):
                    wrow = pl.multiple_of(z * BX + 8 * xt, 8)
                    w = [WM[pl.ds(i * WR + wrow, 8), :] for i in range(6)]
                    c6 = C6[pl.ds(wrow, 8), :]
                    for r in range(R):
                        ring = now + 16 * ((k * XT + xt) * R + r)
                        row = pl.multiple_of(tile_row(r, z, xt), 8)
                        at = base + row
                        low = RING[pl.ds(ring, 8), :]
                        high = RING[pl.ds(ring + 8, 8), :]
                        beside = w[0] * F[pl.ds(at - 1, 8), :] + w[1] * F[pl.ds(at + 1, 8), :]
                        beside = beside + (w[2] * low + w[3] * high)
                        beside = beside + (
                            w[4] * F[pl.ds(at - BX, 8), :] + w[5] * F[pl.ds(at + BX, 8), :]
                        )
                        stores.append((out + row, c6 * F[pl.ds(at, 8), :] - beside))
            places = [(step * GROUP + k, xt) for k in range(GROUP) for xt in range(XT)]
            for lev, other, start, pairs in groups:
                where = [pl.ds(8 * (start + index), 8) for index in range(len(pairs))]
                acc = [ACC[w, :] for w in where]
                products(lev, other, pairs, places, acc)
                for w, value in zip(where, acc):
                    ACC[w, :] = value
            for at, value in stores:
                W[pl.ds(at, 8), :] = value
            for at, value in kept:
                RING[pl.ds(at, 8), :] = value
            return carry

        lax.fori_loop(0, STEPS, body, 0)
        for _, _, start, pairs in groups:
            fold([ACC[pl.ds(8 * (start + index), 8), :] for index in range(len(pairs))], start)

    def correct(level, half):
        out = max(level - 1, 0) * FR
        ahead = (level + 1) * FS + PAD
        even = (lane & 1) == 0
        halos = [
            jnp.where(
                even,
                pltpu.roll(HY[level, half, 0, pl.ds(8 * xt, 8), :], 1, 1),
                pltpu.roll(HY[level, half, 1, pl.ds(8 * xt, 8), :], L - 1, 1),
            )
            for xt in range(XT)
        ]
        acc = [zero] * XT
        for zh in range(HALF):
            z = half * HALF + zh
            for xt, r in tiles:
                row = tile_row(r, z, xt)
                halo = pltpu.roll(halos[xt], (L - pack_lane(r, zh)) % L, 1)
                image = W[pl.ds(out + row, 8), :] - WE[pl.ds(z * BX + 8 * xt, 8), :] * halo
                for side, where in ((0, 0), (1, XT - 1)):
                    if xt == where:
                        edge_x = WX[pl.ds((side * NZ + z) * 8, 8), :]
                        halo_x = HX[level, half, side, pl.ds(r * HALF + zh, 1), :]
                        image = image - edge_x * jnp.broadcast_to(halo_x, (8, L))
                if level == 0:
                    following = B[pl.ds(row, 8), :] - image
                else:
                    W[pl.ds(out + row, 8), :] = image
                    held = F[pl.ds(level * FS + PAD + row, 8), :]
                    following = image * (1.0 / SCALE_DOWN) - held * (
                        SHIFTS[level - 1] / SCALE_DOWN
                    )
                if level < 4:
                    F[pl.ds(ahead + row, 8), :] = following
                    for side, where, take in ((0, 0, 0), (1, XT - 1, 7)):
                        if xt == where:
                            XS[level + 1, half, side, pl.ds(r * HALF + zh, 1), :] = (
                                following[take : take + 1]
                            )
                    acc[xt] = pack_tile(following, r, zh, acc[xt])
        if half and level < 4:
            first_rolls(level + 1)
        return acc

    def combine(a, b, d):
        mask = (sub & d) == 0
        return jnp.where(mask, a, b) + pltpu.roll(jnp.where(mask, b, a), d, 0)

    def gram(level):
        for lev, other, start, pairs in GROUPS:
            if lev != level:
                continue

            def body(step, acc):
                acc = list(acc)
                places = [(2 * step + k, xt) for k in range(2) for xt in range(XT)]
                products(lev, other, pairs, places, acc)
                return tuple(acc)

            fold(list(lax.fori_loop(0, NZ // 2, body, (zero,) * len(pairs))), start)

    for copy in loads[0]:
        copy.wait()
    for copy in loads[3]:
        copy.start()

    packed = []
    for half in range(2):
        def pack_body(step, acc, half=half):
            acc = list(acc)
            for k in range(GROUP):
                zh = step * GROUP + k
                for xt, r in tiles:
                    row = pl.multiple_of(PAD + tile_row(r, half * HALF + zh, xt), 8)
                    tile = F[pl.ds(row, 8), :]
                    acc[xt] = pack_tile(tile, r, zh, acc[xt])
                    for side, where, take in ((0, 0, 0), (1, XT - 1, 7)):
                        if xt == where:
                            XS[0, half, side, pl.ds(r * HALF + zh, 1), :] = tile[take : take + 1]
            return tuple(acc)

        packed.append(lax.fori_loop(0, HALF // GROUP, pack_body, (zero,) * XT))
    pl.semaphore_wait(barrier, len(hello) + len(inner_peers) + len(outer_peers))
    for half in range(2):
        send(0, half, packed[half])

    for copy in loads[1] + loads[2]:
        copy.wait()

    def prepare(z, carry):
        stores = []
        for xt in range(XT):
            row = pl.multiple_of(z * BX + 8 * xt, 8)
            stores.append((C6, row, C6[pl.ds(row, 8), :] + 6.0))
            for side, where, inside in ((0, 0, sub != 0), (1, XT - 1, sub != 7)):
                if xt == where:
                    w = WM[pl.ds(side * WR + row, 8), :]
                    stores.append((WM, side * WR + row, jnp.where(inside, w, 0.0)))
                    at = pl.multiple_of((side * NZ + z) * 8, 8)
                    stores.append((WX, at, jnp.where(inside, 0.0, w)))
            low = WM[pl.ds(2 * WR + row, 8), :]
            high = WM[pl.ds(3 * WR + row, 8), :]
            edge = jnp.where(lane == 0, low, jnp.where(lane == L - 1, high, 0.0))
            stores.append((WE, row, edge))
            stores.append((WM, 2 * WR + row, jnp.where(lane == 0, 0.0, low)))
            stores.append((WM, 3 * WR + row, jnp.where(lane == L - 1, 0.0, high)))
        for ref, at, value in stores:
            ref[pl.ds(at, 8), :] = value
        return carry

    lax.fori_loop(0, NZ, prepare, 0)
    for xt in range(XT):
        WM[pl.ds(4 * WR + 8 * xt, 8), :] = zero
        WM[pl.ds(5 * WR + (NZ - 1) * BX + 8 * xt, 8), :] = zero
    first_rolls(0)
    bulk(0)
    for copy in loads[3]:
        copy.wait()
    for level in range(5):
        for half in range(2):
            receive(level, half)
            acc = correct(level, half)
            if level < 4:
                send(level + 1, half, acc)
        if level < 4:
            bulk(level + 1, level - 1)
        sent(level)
    gram(3)

    for q in range(USED, LANES, 8):
        RED[pl.ds(q, 8), :] = zero
    total = lax.dot_general(
        jnp.ones((8, L), jnp.float32), RED[...], (((1,), (1,)), ((), ())),
        precision=lax.Precision.HIGHEST, preferred_element_type=jnp.float32,
    )

    def exchange(total, buffer, peers, send_sems, recv_sems):
        buffer[pl.ds(0, 8), :] = total
        copies = []
        for k, peer in enumerate(peers):
            copy = pltpu.make_async_remote_copy(
                src_ref=buffer.at[pl.ds(0, 2)], dst_ref=buffer.at[pl.ds(8 + 2 * k, 2)],
                send_sem=send_sems.at[k], recv_sem=recv_sems.at[k],
                device_id=peer, device_id_type=MESH,
            )
            copy.start()
            copies.append(copy)
        own = jnp.where(sub < 2, total, 0.0)
        for copy in copies:
            copy.wait_recv()
        parts = [own]
        for at in range(0, 2 * len(peers), 8):
            part = buffer[pl.ds(8 + at, 8), :]
            left = 2 * len(peers) - at
            parts.append(part if left >= 8 else jnp.where(sub < left, part, 0.0))
        while len(parts) > 1:
            parts = [
                parts[k] + parts[k + 1] if k + 1 < len(parts) else parts[k]
                for k in range(0, len(parts), 2)
            ]
        for copy in copies:
            copy.wait_send()
        total = parts[0]
        for d in (2, 4):
            total = total + pltpu.roll(total, d, 0)
        return total

    total = jnp.where((sub & 1) == 0, total[:, :L], total[:, L:])
    total = exchange(total, RA, inner_peers, sa, ra)
    total = exchange(total, RB, outer_peers, sb, rb)
    swapped = pltpu.roll(total, 1, 0)
    even_row = (sub & 1) == 0
    total = [jnp.where(even_row, total, swapped), jnp.where(even_row, swapped, total)]

    def entry(p):
        return jnp.broadcast_to(total[p // L][:, p % L : p % L + 1], (8, L))

    order = 16
    A = {}
    for i in range(order):
        for j in range(i + 1):
            A[i, j] = entry(TABLE[(i // R, i % R, j // R, j % R)])
    rhs = []
    for i in range(order):
        column = [entry(TABLE[(i // R, i % R, 4, r)]) for r in range(R)]
        rhs.append(
            jnp.where(sub == 0, column[0],
                      jnp.where(sub == 1, column[1],
                                jnp.where(sub == 2, column[2], column[3])))
        )
    lower, inverse = {}, []
    for k in range(order):
        inv = 1.0 / A[k, k]
        inverse.append(inv)
        for i in range(k + 1, order):
            lower[i, k] = A[i, k] * inv
        for i in range(k + 1, order):
            for j in range(k + 1, i + 1):
                A[i, j] = A[i, j] - lower[i, k] * A[j, k]
            rhs[i] = rhs[i] - lower[i, k] * rhs[k]
    coeffs = [None] * order
    for k in range(order - 1, -1, -1):
        value = rhs[k] * inverse[k]
        for i in range(order - 1, k, -1):
            value = value - lower[i, k] * coeffs[i]
        coeffs[k] = value
        for r in range(R):
            CS[pl.ds((r * order + k) * 8, 8), :] = jnp.broadcast_to(value[r : r + 1], (8, L))


UPDATE_STEPS = 8


def update(F, W, CS, sol_hbm, res_hbm, sol, res, sems):
    planes = NZ // UPDATE_STEPS

    def writes(step):
        where = (slice(None), pl.ds(step * planes, planes))
        return [
            pltpu.make_async_copy(source.at[where], target.at[where], sems.at[k, step])
            for k, (source, target) in enumerate(((sol, sol_hbm), (res, res_hbm)))
        ]

    def body(step, carry):
        def plane(k, carry):
            z = step * planes + k
            sums = []
            for r in range(R):
                for xt in range(XT):
                    row = pl.multiple_of((r * NZ + z) * BX + 8 * xt, 8)
                    sums.append([F[pl.ds(f * FS + PAD + row, 8), :] for f in range(2)])
            for i in range(16):
                coef = [CS[pl.ds((r * 16 + i) * 8, 8), :] for r in range(R)]
                for xt in range(XT):
                    row = pl.multiple_of(((i % R) * NZ + z) * BX + 8 * xt, 8)
                    basis = F[pl.ds((i // R + 1) * FS + PAD + row, 8), :]
                    image = W[pl.ds((i // R) * FR + row, 8), :]
                    for r in range(R):
                        both = sums[r * XT + xt]
                        both[0] = both[0] + coef[r] * basis
                        both[1] = both[1] - coef[r] * image
            for r in range(R):
                for xt in range(XT):
                    sol[r, z, pl.ds(8 * xt, 8), :] = sums[r * XT + xt][0]
                    res[r, z, pl.ds(8 * xt, 8), :] = sums[r * XT + xt][1]
            return carry

        lax.fori_loop(0, planes, plane, 0)
        for copy in writes(step):
            copy.start()
        return carry

    lax.fori_loop(0, UPDATE_STEPS, body, 0)
    for step in range(UPDATE_STEPS):
        for copy in writes(step):
            copy.wait()


def on_device(gx_size, gy_size, right_side, start_field, center, weights):
    inner = min(8, gx_size // 2)
    outer = gx_size // inner
    dma = pltpu.SemaphoreType.DMA
    f32 = jnp.float32
    flat = lambda a: a.reshape(-1, L)
    held = pltpu.MemorySpace.VMEM
    rows_for = lambda devices: 8 + (2 * devices + 5) // 8 * 8
    shape = lambda *dims: jax.ShapeDtypeStruct(dims, f32)
    in_hbm = lambda a: pltpu.with_memory_space_constraint(flat(a), pltpu.HBM)
    fields, images, coeffs = pl.pallas_call(
        functools.partial(kernel, gx_size, gy_size, inner),
        out_shape=[shape(5 * FS, L), shape(4 * FR, L), shape(64 * 8, L)],
        in_specs=[pl.BlockSpec(memory_space=pltpu.HBM)] * 4,
        out_specs=[pl.BlockSpec(memory_space=held)] * 3,
        scratch_shapes=[
            pltpu.VMEM((FR, L), f32),
            pltpu.VMEM((WR, L), f32),
            pltpu.VMEM((6 * WR, L), f32),
            pltpu.VMEM((WR, L), f32),
            pltpu.VMEM((2 * NZ * 8, L), f32),
            pltpu.VMEM((5, 2, 2, R * HALF, L), f32),
            pltpu.VMEM((5, 2, 2, BX, L), f32),
            pltpu.VMEM((5, 2, 2, R * HALF, L), f32),
            pltpu.VMEM((5, 2, BX, L), f32),
            pltpu.VMEM((2 * 2 * GROUP * R * XT * 8, L), f32),
            pltpu.VMEM((8 * USED, L), f32),
            pltpu.VMEM((LANES, L), f32),
            pltpu.VMEM((rows_for(inner), L), f32),
            pltpu.VMEM((rows_for(outer * gy_size), L), f32),
            dma((4, 6)),
            dma((5, 2, 2)), dma((5, 2, 2)), dma((5, 2, 2)), dma((5, 2, 2)),
            dma((inner,)), dma((inner,)),
            dma((outer * gy_size,)), dma((outer * gy_size,)),
        ],
        compiler_params=pltpu.CompilerParams(
            collective_id=0, has_side_effects=True, vmem_limit_bytes=32 * 1024 * 1024,
        ),
    )(in_hbm(right_side), in_hbm(start_field), in_hbm(center), in_hbm(weights))
    return pl.pallas_call(
        update,
        out_shape=[shape(R, NZ, BX, L)] * 2,
        in_specs=[pl.BlockSpec(memory_space=held)] * 3,
        out_specs=[pl.BlockSpec(memory_space=pltpu.HBM)] * 2,
        scratch_shapes=[pltpu.VMEM((R, NZ, BX, L), f32)] * 2 + [dma((2, UPDATE_STEPS))],
        compiler_params=pltpu.CompilerParams(vmem_limit_bytes=16 * 1024 * 1024),
    )(fields, images, coeffs)


def solution(mesh):
    gx_size, gy_size = mesh.shape["gx"], mesh.shape["gy"]
    return jax.shard_map(
        functools.partial(on_device, gx_size, gy_size),
        mesh=mesh,
        in_specs=(
            P(None, None, "gx", "gy"),
            P(None, None, "gx", "gy"),
            P(None, "gx", "gy"),
            P(None, None, "gx", "gy"),
        ),
        out_specs=(P(None, None, "gx", "gy"), P(None, None, "gx", "gy")),
        check_vma=False,
    )
```

```python
import functools

import jax
import jax.numpy as jnp
from jax import lax
from jax.experimental import pallas as pl
from jax.experimental.pallas import tpu as pltpu
from jax.sharding import PartitionSpec as P

SHIFTS = (12.0, 2.0, 8.0, 5.0)
SCALE_DOWN = 5.0
MESH = pl.DeviceIdType.MESH

R, NZ, BX, L = 4, 24, 24, 128
XT = BX // 8
FR = R * NZ * BX
WR = NZ * BX
PAD = 24
FS = FR + 2 * PAD
HALF = NZ // 2
GROUP = 4
STEPS = NZ // GROUP


def pair_table():
    table, groups, at = {}, [], 0
    for level in range(4):
        for other in (level, 4) + tuple(range(level)):
            pairs = [
                (a, b)
                for a in range(R)
                for b in range(R)
                if other != level or b <= a
            ]
            for index, (a, b) in enumerate(pairs):
                table[(level, a, other, b)] = at + index
            groups.append((level, other, at, pairs))
            at += (len(pairs) + 7) // 8 * 8
    return table, groups, at


TABLE, GROUPS, USED = pair_table()
LANES = 256


def kernel(
    gx_size, gy_size, inner,
    b_hbm, x0_hbm, c_hbm, w_hbm,
    F, W, CS,
    B, C6, WM, WE, WX, HX, HY, XS, YS, RING, ACC, RED, RA, RB,
    ld, sx, rx, sy, ry, sa, ra, sb, rb,
):
    gx = lax.axis_index("gx")
    gy = lax.axis_index("gy")
    outer = gx_size // inner
    base_x = (gx // inner) * inner
    in_x = gx - base_x

    loads = [[], [], [], []]
    for group, (source, ref, offset, parts) in enumerate((
        (x0_hbm, F, PAD, R), (w_hbm, WM, 0, 6), (c_hbm, C6, 0, 1), (b_hbm, B, 0, R),
    )):
        rows = source.shape[0] // parts
        for part in range(parts):
            copy = pltpu.make_async_copy(
                source.at[pl.ds(part * rows, rows)],
                ref.at[pl.ds(offset + part * rows, rows)],
                ld.at[group, part],
            )
            loads[group].append(copy)
    for copy in loads[0] + loads[2] + loads[1]:
        copy.start()

    barrier = pltpu.get_barrier_semaphore()
    hello = []
    for step in (1, gx_size - 1):
        hello.append((lax.rem(gx + step, gx_size), gy))
    for step in (1, gy_size - 1):
        hello.append((gx, lax.rem(gy + step, gy_size)))
    inner_peers = [(base_x + lax.rem(in_x + i, inner), gy) for i in range(1, inner)]
    outer_peers = []
    for i in range(outer):
        for j in range(gy_size):
            if i or j:
                outer_peers.append(
                    (lax.rem(gx + i * inner, gx_size), lax.rem(gy + j, gy_size))
                )
    for peer in hello + inner_peers + outer_peers:
        pl.semaphore_signal(barrier, inc=1, device_id=peer, device_id_type=MESH)

    zero = jnp.zeros((8, L), jnp.float32)
    lane = lax.broadcasted_iota(jnp.int32, (8, L), 1)
    sub = lax.broadcasted_iota(jnp.int32, (8, L), 0)
    first_x, last_x = gx == 0, gx == gx_size - 1
    first_y, last_y = gy == 0, gy == gy_size - 1
    for f in range(5):
        for p in range(3):
            F[pl.ds(f * FS + 8 * p, 8), :] = zero
            F[pl.ds(f * FS + PAD + FR + 8 * p, 8), :] = zero

    tiles = [(xt, r) for xt in range(XT) for r in range(R)]

    def tile_row(r, z, xt):
        return (r * NZ + z) * BX + 8 * xt

    def aligned(row):
        return row if isinstance(row, int) else pl.multiple_of(row, 8)

    def pack_lane(r, zh):
        return 2 * (r * HALF + zh)

    def pack_tile(tile, r, zh, acc):
        j2 = pack_lane(r, zh)
        mask = ((lane + (1 - j2)) & (L - 1)) < 2
        return jnp.where(mask, pltpu.roll(tile, j2, 1), acc)

    up_x, down_x = (lax.rem(gx + 1, gx_size), gy), (lax.rem(gx + gx_size - 1, gx_size), gy)
    up_y, down_y = (gx, lax.rem(gy + 1, gy_size)), (gx, lax.rem(gy + gy_size - 1, gy_size))

    def copies_x(level, half):
        return [
            pltpu.make_async_remote_copy(
                src_ref=XS.at[level, half, 1 - lands], dst_ref=HX.at[level, half, lands],
                send_sem=sx.at[level, half, lands], recv_sem=rx.at[level, half, lands],
                device_id=peer, device_id_type=MESH)
            for lands, peer in enumerate((up_x, down_x))
        ]

    def copies_y(level, half):
        return [
            pltpu.make_async_remote_copy(
                src_ref=YS.at[level, half], dst_ref=HY.at[level, half, lands],
                send_sem=sy.at[level, half, lands], recv_sem=ry.at[level, half, lands],
                device_id=peer, device_id_type=MESH)
            for lands, peer in enumerate((up_y, down_y))
        ]

    def send_x(level, half):
        for copy in copies_x(level, half):
            copy.start()

    def send_y(level, half, acc):
        for xt in range(XT):
            YS[level, half, pl.ds(8 * xt, 8), :] = acc[xt]
        for copy in copies_y(level, half):
            copy.start()

    def receive(level, half):
        for copy in copies_y(level, half) + copies_x(level, half):
            copy.wait_recv()

    def sent(level):
        for half in range(2):
            for copy in copies_x(level, half) + copies_y(level, half):
                copy.wait_send()

    slot = 2 * GROUP * R * XT * 8

    def keep_rolls(level, z0, at):
            base = level * FS + PAD
            kept = []
            for k in range(GROUP):
                for index, (xt, r) in enumerate(tiles):
                    mid = F[pl.ds(aligned(base + tile_row(r, z0 + k, xt)), 8), :]
                    where = at + 16 * (k * R * XT + index)
                    kept.append((where, pltpu.roll(mid, 1, 1)))
                    kept.append((where + 8, pltpu.roll(mid, L - 1, 1)))
            return kept

    def first_rolls(level):
        for at, value in keep_rolls(level, 0, 0):
            RING[pl.ds(at, 8), :] = value

    def rows_of(block, r, z, xt):
        row = aligned(tile_row(r, z, xt))
        if block == 4:
            return F[pl.ds(FS + PAD + row, 8), :]
        return W[pl.ds(block * FR + row, 8), :]

    def products(lev, other, pairs, places, acc):
        for z, xt in places:
            left = [rows_of(lev, r, z, xt) for r in range(R)]
            right = left if other == lev else [rows_of(other, r, z, xt) for r in range(R)]
            for index, (a, b) in enumerate(pairs):
                acc[index] = acc[index] + left[a] * right[b]

    def fold(sums, start):
        sums = sums + [zero] * (-len(sums) % 8)
        for q in range(0, len(sums), 8):
            part = sums[q : q + 8]
            for d in (1, 2, 4):
                part = [combine(part[k], part[k + 1], d) for k in range(0, len(part), 2)]
            RED[pl.ds(start + q, 8), :] = part[0]

    def bulk(level, gram_level=None):
        base = level * FS + PAD
        out = max(level - 1, 0) * FR
        groups = [g for g in GROUPS if g[0] == gram_level]
        for _, _, start, pairs in groups:
            for index in range(len(pairs)):
                ACC[pl.ds(8 * (start + index), 8), :] = zero

        def body(step, carry):
            now = pl.multiple_of(lax.rem(step, 2) * slot, 8)
            later = pl.multiple_of(slot - now, 8)
            kept = keep_rolls(level, jnp.minimum(step + 1, STEPS - 1) * GROUP, later)
            stores = []
            for k in range(GROUP):
                z = step * GROUP + k
                for xt in range(XT):
                    wrow = pl.multiple_of(z * BX + 8 * xt, 8)
                    w = [WM[pl.ds(i * WR + wrow, 8), :] for i in range(6)]
                    c6 = C6[pl.ds(wrow, 8), :]
                    for r in range(R):
                        ring = now + 16 * ((k * XT + xt) * R + r)
                        row = pl.multiple_of(tile_row(r, z, xt), 8)
                        at = base + row
                        low = RING[pl.ds(ring, 8), :]
                        high = RING[pl.ds(ring + 8, 8), :]
                        beside = w[0] * F[pl.ds(at - 1, 8), :] + w[1] * F[pl.ds(at + 1, 8), :]
                        beside = beside + (w[2] * low + w[3] * high)
                        beside = beside + (
                            w[4] * F[pl.ds(at - BX, 8), :] + w[5] * F[pl.ds(at + BX, 8), :]
                        )
                        stores.append((out + row, c6 * F[pl.ds(at, 8), :] - beside))
            places = [(step * GROUP + k, xt) for k in range(GROUP) for xt in range(XT)]
            for lev, other, start, pairs in groups:
                where = [pl.ds(8 * (start + index), 8) for index in range(len(pairs))]
                acc = [ACC[w, :] for w in where]
                products(lev, other, pairs, places, acc)
                for w, value in zip(where, acc):
                    ACC[w, :] = value
            for at, value in stores:
                W[pl.ds(at, 8), :] = value
            for at, value in kept:
                RING[pl.ds(at, 8), :] = value
            return carry

        lax.fori_loop(0, STEPS, body, 0)
        for _, _, start, pairs in groups:
            fold([ACC[pl.ds(8 * (start + index), 8), :] for index in range(len(pairs))], start)

    def correct(level, half):
        out = max(level - 1, 0) * FR
        ahead = (level + 1) * FS + PAD
        even = (lane & 1) == 0
        halos = [
            jnp.where(
                even,
                pltpu.roll(HY[level, half, 0, pl.ds(8 * xt, 8), :], 1, 1),
                pltpu.roll(HY[level, half, 1, pl.ds(8 * xt, 8), :], L - 1, 1),
            )
            for xt in range(XT)
        ]
        def plane(zh, xt):
            z = half * HALF + zh
            for r in range(R):
                row = tile_row(r, z, xt)
                halo = pltpu.roll(halos[xt], (L - pack_lane(r, zh)) % L, 1)
                image = W[pl.ds(out + row, 8), :] - WE[pl.ds(z * BX + 8 * xt, 8), :] * halo
                for side, where in ((0, 0), (1, XT - 1)):
                    if xt == where:
                        edge_x = WX[pl.ds((side * NZ + z) * 8, 8), :]
                        halo_x = HX[level, half, side, pl.ds(r * HALF + zh, 1), :]
                        image = image - edge_x * jnp.broadcast_to(halo_x, (8, L))
                if level == 0:
                    following = B[pl.ds(row, 8), :] - image
                else:
                    W[pl.ds(out + row, 8), :] = image
                    held = F[pl.ds(level * FS + PAD + row, 8), :]
                    following = image * (1.0 / SCALE_DOWN) - held * (
                        SHIFTS[level - 1] / SCALE_DOWN
                    )
                if level < 4:
                    F[pl.ds(ahead + row, 8), :] = following
                    for side, where, take in ((0, 0, 0), (1, XT - 1, 7)):
                        if xt == where:
                            XS[level + 1, half, side, pl.ds(r * HALF + zh, 1), :] = (
                                following[take : take + 1]
                            )

        for zh in range(HALF):
            plane(zh, 0)
            plane(zh, XT - 1)
        if level < 4:
            send_x(level + 1, half)
        for zh in range(HALF):
            for xt in range(1, XT - 1):
                plane(zh, xt)
        if level < 4:
            acc = [zero] * XT
            for zh in range(HALF):
                for xt, r in tiles:
                    row = tile_row(r, half * HALF + zh, xt)
                    acc[xt] = pack_tile(F[pl.ds(ahead + row, 8), :], r, zh, acc[xt])
            send_y(level + 1, half, acc)
        if half and level < 4:
            first_rolls(level + 1)

    def combine(a, b, d):
        mask = (sub & d) == 0
        return jnp.where(mask, a, b) + pltpu.roll(jnp.where(mask, b, a), d, 0)

    def gram(level):
        for lev, other, start, pairs in GROUPS:
            if lev != level:
                continue

            def body(step, acc):
                acc = list(acc)
                places = [(2 * step + k, xt) for k in range(2) for xt in range(XT)]
                products(lev, other, pairs, places, acc)
                return tuple(acc)

            fold(list(lax.fori_loop(0, NZ // 2, body, (zero,) * len(pairs))), start)

    for copy in loads[0]:
        copy.wait()
    for copy in loads[3]:
        copy.start()

    packed = []
    for half in range(2):
        def pack_body(step, acc, half=half):
            acc = list(acc)
            for k in range(GROUP):
                zh = step * GROUP + k
                for xt, r in tiles:
                    row = pl.multiple_of(PAD + tile_row(r, half * HALF + zh, xt), 8)
                    tile = F[pl.ds(row, 8), :]
                    acc[xt] = pack_tile(tile, r, zh, acc[xt])
                    for side, where, take in ((0, 0, 0), (1, XT - 1, 7)):
                        if xt == where:
                            XS[0, half, side, pl.ds(r * HALF + zh, 1), :] = tile[take : take + 1]
            return tuple(acc)

        packed.append(lax.fori_loop(0, HALF // GROUP, pack_body, (zero,) * XT))
    pl.semaphore_wait(barrier, len(hello) + len(inner_peers) + len(outer_peers))
    for half in range(2):
        send_x(0, half)
        send_y(0, half, packed[half])

    for copy in loads[1] + loads[2]:
        copy.wait()

    def prepare(z, carry):
        stores = []
        for xt in range(XT):
            row = pl.multiple_of(z * BX + 8 * xt, 8)
            stores.append((C6, row, C6[pl.ds(row, 8), :] + 6.0))
            for side, where, inside, ends in (
                (0, 0, sub != 0, first_x), (1, XT - 1, sub != 7, last_x)
            ):
                if xt == where:
                    w = WM[pl.ds(side * WR + row, 8), :]
                    stores.append((WM, side * WR + row, jnp.where(inside, w, 0.0)))
                    at = pl.multiple_of((side * NZ + z) * 8, 8)
                    stores.append((WX, at, jnp.where(inside | ends, 0.0, w)))
            low = WM[pl.ds(2 * WR + row, 8), :]
            high = WM[pl.ds(3 * WR + row, 8), :]
            edge = jnp.where((lane == 0) & jnp.logical_not(first_y), low, 0.0)
            edge = jnp.where((lane == L - 1) & jnp.logical_not(last_y), high, edge)
            stores.append((WE, row, edge))
            stores.append((WM, 2 * WR + row, jnp.where(lane == 0, 0.0, low)))
            stores.append((WM, 3 * WR + row, jnp.where(lane == L - 1, 0.0, high)))
        for ref, at, value in stores:
            ref[pl.ds(at, 8), :] = value
        return carry

    lax.fori_loop(0, NZ, prepare, 0)
    for xt in range(XT):
        WM[pl.ds(4 * WR + 8 * xt, 8), :] = zero
        WM[pl.ds(5 * WR + (NZ - 1) * BX + 8 * xt, 8), :] = zero
    first_rolls(0)
    bulk(0)
    for copy in loads[3]:
        copy.wait()
    for level in range(5):
        for half in range(2):
            receive(level, half)
            correct(level, half)
        if level < 4:
            bulk(level + 1, level - 1)
        sent(level)
    gram(3)

    for q in range(USED, LANES, 8):
        RED[pl.ds(q, 8), :] = zero
    total = lax.dot_general(
        jnp.ones((8, L), jnp.float32), RED[...], (((1,), (1,)), ((), ())),
        precision=lax.Precision.HIGHEST, preferred_element_type=jnp.float32,
    )

    def exchange(total, buffer, peers, send_sems, recv_sems):
        buffer[pl.ds(0, 8), :] = total
        copies = []
        for k, peer in enumerate(peers):
            copy = pltpu.make_async_remote_copy(
                src_ref=buffer.at[pl.ds(0, 2)], dst_ref=buffer.at[pl.ds(8 + 2 * k, 2)],
                send_sem=send_sems.at[k], recv_sem=recv_sems.at[k],
                device_id=peer, device_id_type=MESH,
            )
            copy.start()
            copies.append(copy)
        own = jnp.where(sub < 2, total, 0.0)
        for copy in copies:
            copy.wait_recv()
        parts = [own]
        for at in range(0, 2 * len(peers), 8):
            part = buffer[pl.ds(8 + at, 8), :]
            left = 2 * len(peers) - at
            parts.append(part if left >= 8 else jnp.where(sub < left, part, 0.0))
        while len(parts) > 1:
            parts = [
                parts[k] + parts[k + 1] if k + 1 < len(parts) else parts[k]
                for k in range(0, len(parts), 2)
            ]
        for copy in copies:
            copy.wait_send()
        total = parts[0]
        for d in (2, 4):
            total = total + pltpu.roll(total, d, 0)
        return total

    total = jnp.where((sub & 1) == 0, total[:, :L], total[:, L:])
    total = exchange(total, RA, inner_peers, sa, ra)
    total = exchange(total, RB, outer_peers, sb, rb)
    swapped = pltpu.roll(total, 1, 0)
    even_row = (sub & 1) == 0
    total = [jnp.where(even_row, total, swapped), jnp.where(even_row, swapped, total)]

    def entry(p):
        return jnp.broadcast_to(total[p // L][:, p % L : p % L + 1], (8, L))

    order = 16
    A = {}
    for i in range(order):
        for j in range(i + 1):
            A[i, j] = entry(TABLE[(i // R, i % R, j // R, j % R)])
    rhs = []
    for i in range(order):
        column = [entry(TABLE[(i // R, i % R, 4, r)]) for r in range(R)]
        rhs.append(
            jnp.where(sub == 0, column[0],
                      jnp.where(sub == 1, column[1],
                                jnp.where(sub == 2, column[2], column[3])))
        )
    lower, inverse = {}, []
    for k in range(order):
        inv = 1.0 / A[k, k]
        inverse.append(inv)
        for i in range(k + 1, order):
            lower[i, k] = A[i, k] * inv
        for i in range(k + 1, order):
            for j in range(k + 1, i + 1):
                A[i, j] = A[i, j] - lower[i, k] * A[j, k]
            rhs[i] = rhs[i] - lower[i, k] * rhs[k]
    coeffs = [None] * order
    for k in range(order - 1, -1, -1):
        value = rhs[k] * inverse[k]
        for i in range(order - 1, k, -1):
            value = value - lower[i, k] * coeffs[i]
        coeffs[k] = value
        for r in range(R):
            CS[pl.ds((r * order + k) * 8, 8), :] = jnp.broadcast_to(value[r : r + 1], (8, L))


UPDATE_STEPS = 8


def update(F, W, CS, sol_hbm, res_hbm, sol, res, sems):
    planes = NZ // UPDATE_STEPS

    def writes(step):
        where = (slice(None), pl.ds(step * planes, planes))
        return [
            pltpu.make_async_copy(source.at[where], target.at[where], sems.at[k, step])
            for k, (source, target) in enumerate(((sol, sol_hbm), (res, res_hbm)))
        ]

    def body(step, carry):
        def plane(k, carry):
            z = step * planes + k
            sums = []
            for r in range(R):
                for xt in range(XT):
                    row = pl.multiple_of((r * NZ + z) * BX + 8 * xt, 8)
                    sums.append([F[pl.ds(f * FS + PAD + row, 8), :] for f in range(2)])
            for i in range(16):
                coef = [CS[pl.ds((r * 16 + i) * 8, 8), :] for r in range(R)]
                for xt in range(XT):
                    row = pl.multiple_of(((i % R) * NZ + z) * BX + 8 * xt, 8)
                    basis = F[pl.ds((i // R + 1) * FS + PAD + row, 8), :]
                    image = W[pl.ds((i // R) * FR + row, 8), :]
                    for r in range(R):
                        both = sums[r * XT + xt]
                        both[0] = both[0] + coef[r] * basis
                        both[1] = both[1] - coef[r] * image
            for r in range(R):
                for xt in range(XT):
                    sol[r, z, pl.ds(8 * xt, 8), :] = sums[r * XT + xt][0]
                    res[r, z, pl.ds(8 * xt, 8), :] = sums[r * XT + xt][1]
            return carry

        lax.fori_loop(0, planes, plane, 0)
        for copy in writes(step):
            copy.start()
        return carry

    lax.fori_loop(0, UPDATE_STEPS, body, 0)
    for step in range(UPDATE_STEPS):
        for copy in writes(step):
            copy.wait()


def on_device(gx_size, gy_size, right_side, start_field, center, weights):
    inner = min(8, gx_size // 2)
    outer = gx_size // inner
    dma = pltpu.SemaphoreType.DMA
    f32 = jnp.float32
    flat = lambda a: a.reshape(-1, L)
    held = pltpu.MemorySpace.VMEM
    rows_for = lambda devices: 8 + (2 * devices + 5) // 8 * 8
    shape = lambda *dims: jax.ShapeDtypeStruct(dims, f32)
    in_hbm = lambda a: pltpu.with_memory_space_constraint(flat(a), pltpu.HBM)
    fields, images, coeffs = pl.pallas_call(
        functools.partial(kernel, gx_size, gy_size, inner),
        out_shape=[shape(5 * FS, L), shape(4 * FR, L), shape(64 * 8, L)],
        in_specs=[pl.BlockSpec(memory_space=pltpu.HBM)] * 4,
        out_specs=[pl.BlockSpec(memory_space=held)] * 3,
        scratch_shapes=[
            pltpu.VMEM((FR, L), f32),
            pltpu.VMEM((WR, L), f32),
            pltpu.VMEM((6 * WR, L), f32),
            pltpu.VMEM((WR, L), f32),
            pltpu.VMEM((2 * NZ * 8, L), f32),
            pltpu.VMEM((5, 2, 2, R * HALF, L), f32),
            pltpu.VMEM((5, 2, 2, BX, L), f32),
            pltpu.VMEM((5, 2, 2, R * HALF, L), f32),
            pltpu.VMEM((5, 2, BX, L), f32),
            pltpu.VMEM((2 * 2 * GROUP * R * XT * 8, L), f32),
            pltpu.VMEM((8 * USED, L), f32),
            pltpu.VMEM((LANES, L), f32),
            pltpu.VMEM((rows_for(inner), L), f32),
            pltpu.VMEM((rows_for(outer * gy_size), L), f32),
            dma((4, 6)),
            dma((5, 2, 2)), dma((5, 2, 2)), dma((5, 2, 2)), dma((5, 2, 2)),
            dma((inner,)), dma((inner,)),
            dma((outer * gy_size,)), dma((outer * gy_size,)),
        ],
        compiler_params=pltpu.CompilerParams(
            collective_id=0, has_side_effects=True, vmem_limit_bytes=32 * 1024 * 1024,
        ),
    )(in_hbm(right_side), in_hbm(start_field), in_hbm(center), in_hbm(weights))
    return pl.pallas_call(
        update,
        out_shape=[shape(R, NZ, BX, L)] * 2,
        in_specs=[pl.BlockSpec(memory_space=held)] * 3,
        out_specs=[pl.BlockSpec(memory_space=pltpu.HBM)] * 2,
        scratch_shapes=[pltpu.VMEM((R, NZ, BX, L), f32)] * 2 + [dma((2, UPDATE_STEPS))],
        compiler_params=pltpu.CompilerParams(vmem_limit_bytes=16 * 1024 * 1024),
    )(fields, images, coeffs)


def solution(mesh):
    gx_size, gy_size = mesh.shape["gx"], mesh.shape["gy"]
    return jax.shard_map(
        functools.partial(on_device, gx_size, gy_size),
        mesh=mesh,
        in_specs=(
            P(None, None, "gx", "gy"),
            P(None, None, "gx", "gy"),
            P(None, "gx", "gy"),
            P(None, None, "gx", "gy"),
        ),
        out_specs=(P(None, None, "gx", "gy"), P(None, None, "gx", "gy")),
        check_vma=False,
    )
```

```python
import functools

import jax
import jax.numpy as jnp
from jax import lax
from jax.experimental import pallas as pl
from jax.experimental.pallas import tpu as pltpu
from jax.sharding import PartitionSpec as P

SHIFTS = (12.0, 2.0, 8.0, 5.0)
SCALE_DOWN = 5.0
MESH = pl.DeviceIdType.MESH

R, NZ, BX, L = 4, 24, 24, 128
XT = BX // 8
FR = R * NZ * BX
WR = NZ * BX
PAD = 24
FS = FR + 2 * PAD
HALF = NZ // 2
GROUP = 4
STEPS = NZ // GROUP


def pair_table():
    table, groups, at = {}, [], 0
    for level in range(4):
        for other in (level, 4) + tuple(range(level)):
            pairs = [
                (a, b)
                for a in range(R)
                for b in range(R)
                if other != level or b <= a
            ]
            for index, (a, b) in enumerate(pairs):
                table[(level, a, other, b)] = at + index
            groups.append((level, other, at, pairs))
            at += (len(pairs) + 7) // 8 * 8
    return table, groups, at


TABLE, GROUPS, USED = pair_table()
LANES = 256


def kernel(
    gx_size, gy_size, inner,
    b_hbm, x0_hbm, c_hbm, w_hbm,
    F, W, CS,
    B, C6, WM, WE, WX, HX, HY, XS, YS, RING, ACC, RED, RA, RB,
    ld, sx, rx, sy, ry, sa, ra, sb, rb,
):
    gx = lax.axis_index("gx")
    gy = lax.axis_index("gy")
    outer = gx_size // inner
    base_x = (gx // inner) * inner
    in_x = gx - base_x

    loads = [[], [], [], []]
    for group, (source, ref, offset, parts) in enumerate((
        (x0_hbm, F, PAD, R), (w_hbm, WM, 0, 6), (c_hbm, C6, 0, 1), (b_hbm, B, 0, R),
    )):
        rows = source.shape[0] // parts
        for part in range(parts):
            copy = pltpu.make_async_copy(
                source.at[pl.ds(part * rows, rows)],
                ref.at[pl.ds(offset + part * rows, rows)],
                ld.at[group, part],
            )
            loads[group].append(copy)
    for copy in loads[0] + loads[2] + loads[1]:
        copy.start()

    barrier = pltpu.get_barrier_semaphore()
    hello = []
    for step in (1, gx_size - 1):
        hello.append((lax.rem(gx + step, gx_size), gy))
    for step in (1, gy_size - 1):
        hello.append((gx, lax.rem(gy + step, gy_size)))
    inner_peers = [(base_x + lax.rem(in_x + i, inner), gy) for i in range(1, inner)]
    outer_peers = []
    for i in range(outer):
        for j in range(gy_size):
            if i or j:
                outer_peers.append(
                    (lax.rem(gx + i * inner, gx_size), lax.rem(gy + j, gy_size))
                )
    for peer in hello + inner_peers + outer_peers:
        pl.semaphore_signal(barrier, inc=1, device_id=peer, device_id_type=MESH)

    zero = jnp.zeros((8, L), jnp.float32)
    lane = lax.broadcasted_iota(jnp.int32, (8, L), 1)
    sub = lax.broadcasted_iota(jnp.int32, (8, L), 0)
    first_x, last_x = gx == 0, gx == gx_size - 1
    first_y, last_y = gy == 0, gy == gy_size - 1
    for f in range(5):
        for p in range(3):
            F[pl.ds(f * FS + 8 * p, 8), :] = zero
            F[pl.ds(f * FS + PAD + FR + 8 * p, 8), :] = zero

    for cond, ref, side in (
        (first_x, HX, 0), (last_x, HX, 1), (first_y, HY, 0), (last_y, HY, 1),
    ):
        @pl.when(cond)
        def _(ref=ref, side=side):
            for level in range(5):
                for half in range(2):
                    for q in range(ref.shape[3] // 8):
                        ref[level, half, side, pl.ds(8 * q, 8), :] = zero

    tiles = [(xt, r) for xt in range(XT) for r in range(R)]

    def tile_row(r, z, xt):
        return (r * NZ + z) * BX + 8 * xt

    def aligned(row):
        return row if isinstance(row, int) else pl.multiple_of(row, 8)

    def pack_lane(r, zh):
        return 2 * (r * HALF + zh)

    def pack_tile(tile, r, zh, acc):
        j2 = pack_lane(r, zh)
        mask = ((lane + (1 - j2)) & (L - 1)) < 2
        return jnp.where(mask, pltpu.roll(tile, j2, 1), acc)

    up_x, down_x = (lax.rem(gx + 1, gx_size), gy), (lax.rem(gx + gx_size - 1, gx_size), gy)
    up_y, down_y = (gx, lax.rem(gy + 1, gy_size)), (gx, lax.rem(gy + gy_size - 1, gy_size))

    def copies_x(level, half):
        return [
            pltpu.make_async_remote_copy(
                src_ref=XS.at[level, half, 1 - lands], dst_ref=HX.at[level, half, lands],
                send_sem=sx.at[level, half, lands], recv_sem=rx.at[level, half, lands],
                device_id=peer, device_id_type=MESH)
            for lands, peer in enumerate((up_x, down_x))
        ]

    def copies_y(level, half):
        return [
            pltpu.make_async_remote_copy(
                src_ref=YS.at[level, half], dst_ref=HY.at[level, half, lands],
                send_sem=sy.at[level, half, lands], recv_sem=ry.at[level, half, lands],
                device_id=peer, device_id_type=MESH)
            for lands, peer in enumerate((up_y, down_y))
        ]

    def send_x(level, half):
        for missing, copy in zip((last_x, first_x), copies_x(level, half)):
            @pl.when(jnp.logical_not(missing))
            def _(copy=copy):
                copy.start()

    def send_y(level, half, acc):
        for xt in range(XT):
            YS[level, half, pl.ds(8 * xt, 8), :] = acc[xt]
        for missing, copy in zip((last_y, first_y), copies_y(level, half)):
            @pl.when(jnp.logical_not(missing))
            def _(copy=copy):
                copy.start()

    def receive(level, half):
        for missing, copy in zip(
            (first_y, last_y, first_x, last_x), copies_y(level, half) + copies_x(level, half)
        ):
            @pl.when(jnp.logical_not(missing))
            def _(copy=copy):
                copy.wait_recv()

    def sent(level):
        for half in range(2):
            for missing, copy in zip(
                (last_x, first_x, last_y, first_y), copies_x(level, half) + copies_y(level, half)
            ):
                @pl.when(jnp.logical_not(missing))
                def _(copy=copy):
                    copy.wait_send()

    slot = 2 * GROUP * R * XT * 8

    def keep_rolls(level, z0, at):
            base = level * FS + PAD
            kept = []
            for k in range(GROUP):
                for index, (xt, r) in enumerate(tiles):
                    mid = F[pl.ds(aligned(base + tile_row(r, z0 + k, xt)), 8), :]
                    where = at + 16 * (k * R * XT + index)
                    kept.append((where, pltpu.roll(mid, 1, 1)))
                    kept.append((where + 8, pltpu.roll(mid, L - 1, 1)))
            return kept

    def first_rolls(level):
        for at, value in keep_rolls(level, 0, 0):
            RING[pl.ds(at, 8), :] = value

    def rows_of(block, r, z, xt):
        row = aligned(tile_row(r, z, xt))
        if block == 4:
            return F[pl.ds(FS + PAD + row, 8), :]
        return W[pl.ds(block * FR + row, 8), :]

    def products(lev, other, pairs, places, acc):
        for z, xt in places:
            left = [rows_of(lev, r, z, xt) for r in range(R)]
            right = left if other == lev else [rows_of(other, r, z, xt) for r in range(R)]
            for index, (a, b) in enumerate(pairs):
                acc[index] = acc[index] + left[a] * right[b]

    def fold(sums, start):
        sums = sums + [zero] * (-len(sums) % 8)
        for q in range(0, len(sums), 8):
            part = sums[q : q + 8]
            for d in (1, 2, 4):
                part = [combine(part[k], part[k + 1], d) for k in range(0, len(part), 2)]
            RED[pl.ds(start + q, 8), :] = part[0]

    def bulk(level, gram_level=None):
        base = level * FS + PAD
        out = max(level - 1, 0) * FR
        groups = [g for g in GROUPS if g[0] == gram_level]
        for _, _, start, pairs in groups:
            for index in range(len(pairs)):
                ACC[pl.ds(8 * (start + index), 8), :] = zero

        def body(step, carry):
            now = pl.multiple_of(lax.rem(step, 2) * slot, 8)
            later = pl.multiple_of(slot - now, 8)
            kept = keep_rolls(level, jnp.minimum(step + 1, STEPS - 1) * GROUP, later)
            stores = []
            for k in range(GROUP):
                z = step * GROUP + k
                for xt in range(XT):
                    wrow = pl.multiple_of(z * BX + 8 * xt, 8)
                    w = [WM[pl.ds(i * WR + wrow, 8), :] for i in range(6)]
                    c6 = C6[pl.ds(wrow, 8), :]
                    for r in range(R):
                        ring = now + 16 * ((k * XT + xt) * R + r)
                        row = pl.multiple_of(tile_row(r, z, xt), 8)
                        at = base + row
                        low = RING[pl.ds(ring, 8), :]
                        high = RING[pl.ds(ring + 8, 8), :]
                        beside = w[0] * F[pl.ds(at - 1, 8), :] + w[1] * F[pl.ds(at + 1, 8), :]
                        beside = beside + (w[2] * low + w[3] * high)
                        beside = beside + (
                            w[4] * F[pl.ds(at - BX, 8), :] + w[5] * F[pl.ds(at + BX, 8), :]
                        )
                        stores.append((out + row, c6 * F[pl.ds(at, 8), :] - beside))
            places = [(step * GROUP + k, xt) for k in range(GROUP) for xt in range(XT)]
            for lev, other, start, pairs in groups:
                where = [pl.ds(8 * (start + index), 8) for index in range(len(pairs))]
                acc = [ACC[w, :] for w in where]
                products(lev, other, pairs, places, acc)
                for w, value in zip(where, acc):
                    ACC[w, :] = value
            for at, value in stores:
                W[pl.ds(at, 8), :] = value
            for at, value in kept:
                RING[pl.ds(at, 8), :] = value
            return carry

        lax.fori_loop(0, STEPS, body, 0)
        for _, _, start, pairs in groups:
            fold([ACC[pl.ds(8 * (start + index), 8), :] for index in range(len(pairs))], start)

    def correct(level, half):
        out = max(level - 1, 0) * FR
        ahead = (level + 1) * FS + PAD
        even = (lane & 1) == 0
        halos = [
            jnp.where(
                even,
                pltpu.roll(HY[level, half, 0, pl.ds(8 * xt, 8), :], 1, 1),
                pltpu.roll(HY[level, half, 1, pl.ds(8 * xt, 8), :], L - 1, 1),
            )
            for xt in range(XT)
        ]
        def plane(zh, xt):
            z = half * HALF + zh
            for r in range(R):
                row = tile_row(r, z, xt)
                halo = pltpu.roll(halos[xt], (L - pack_lane(r, zh)) % L, 1)
                image = W[pl.ds(out + row, 8), :] - WE[pl.ds(z * BX + 8 * xt, 8), :] * halo
                for side, where in ((0, 0), (1, XT - 1)):
                    if xt == where:
                        edge_x = WX[pl.ds((side * NZ + z) * 8, 8), :]
                        halo_x = HX[level, half, side, pl.ds(r * HALF + zh, 1), :]
                        image = image - edge_x * jnp.broadcast_to(halo_x, (8, L))
                if level == 0:
                    following = B[pl.ds(row, 8), :] - image
                else:
                    W[pl.ds(out + row, 8), :] = image
                    held = F[pl.ds(level * FS + PAD + row, 8), :]
                    following = image * (1.0 / SCALE_DOWN) - held * (
                        SHIFTS[level - 1] / SCALE_DOWN
                    )
                if level < 4:
                    F[pl.ds(ahead + row, 8), :] = following
                    for side, where, take in ((0, 0, 0), (1, XT - 1, 7)):
                        if xt == where:
                            XS[level + 1, half, side, pl.ds(r * HALF + zh, 1), :] = (
                                following[take : take + 1]
                            )

        for zh in range(HALF):
            plane(zh, 0)
            plane(zh, XT - 1)
        if level < 4:
            send_x(level + 1, half)
        for zh in range(HALF):
            for xt in range(1, XT - 1):
                plane(zh, xt)
        if level < 4:
            acc = [zero] * XT
            for zh in range(HALF):
                for xt, r in tiles:
                    row = tile_row(r, half * HALF + zh, xt)
                    acc[xt] = pack_tile(F[pl.ds(ahead + row, 8), :], r, zh, acc[xt])
            send_y(level + 1, half, acc)
        if half and level < 4:
            first_rolls(level + 1)

    def combine(a, b, d):
        mask = (sub & d) == 0
        return jnp.where(mask, a, b) + pltpu.roll(jnp.where(mask, b, a), d, 0)

    def gram(level):
        for lev, other, start, pairs in GROUPS:
            if lev != level:
                continue

            def body(step, acc):
                acc = list(acc)
                places = [(2 * step + k, xt) for k in range(2) for xt in range(XT)]
                products(lev, other, pairs, places, acc)
                return tuple(acc)

            fold(list(lax.fori_loop(0, NZ // 2, body, (zero,) * len(pairs))), start)

    for copy in loads[0]:
        copy.wait()
    for copy in loads[3]:
        copy.start()

    packed = []
    for half in range(2):
        def pack_body(step, acc, half=half):
            acc = list(acc)
            for k in range(GROUP):
                zh = step * GROUP + k
                for xt, r in tiles:
                    row = pl.multiple_of(PAD + tile_row(r, half * HALF + zh, xt), 8)
                    tile = F[pl.ds(row, 8), :]
                    acc[xt] = pack_tile(tile, r, zh, acc[xt])
                    for side, where, take in ((0, 0, 0), (1, XT - 1, 7)):
                        if xt == where:
                            XS[0, half, side, pl.ds(r * HALF + zh, 1), :] = tile[take : take + 1]
            return tuple(acc)

        packed.append(lax.fori_loop(0, HALF // GROUP, pack_body, (zero,) * XT))
    pl.semaphore_wait(barrier, len(hello) + len(inner_peers) + len(outer_peers))
    for half in range(2):
        send_x(0, half)
        send_y(0, half, packed[half])

    for copy in loads[1] + loads[2]:
        copy.wait()

    def prepare(z, carry):
        stores = []
        for xt in range(XT):
            row = pl.multiple_of(z * BX + 8 * xt, 8)
            stores.append((C6, row, C6[pl.ds(row, 8), :] + 6.0))
            for side, where, inside, ends in (
                (0, 0, sub != 0, first_x), (1, XT - 1, sub != 7, last_x)
            ):
                if xt == where:
                    w = WM[pl.ds(side * WR + row, 8), :]
                    stores.append((WM, side * WR + row, jnp.where(inside, w, 0.0)))
                    at = pl.multiple_of((side * NZ + z) * 8, 8)
                    stores.append((WX, at, jnp.where(inside | ends, 0.0, w)))
            low = WM[pl.ds(2 * WR + row, 8), :]
            high = WM[pl.ds(3 * WR + row, 8), :]
            edge = jnp.where((lane == 0) & jnp.logical_not(first_y), low, 0.0)
            edge = jnp.where((lane == L - 1) & jnp.logical_not(last_y), high, edge)
            stores.append((WE, row, edge))
            stores.append((WM, 2 * WR + row, jnp.where(lane == 0, 0.0, low)))
            stores.append((WM, 3 * WR + row, jnp.where(lane == L - 1, 0.0, high)))
        for ref, at, value in stores:
            ref[pl.ds(at, 8), :] = value
        return carry

    lax.fori_loop(0, NZ, prepare, 0)
    for xt in range(XT):
        WM[pl.ds(4 * WR + 8 * xt, 8), :] = zero
        WM[pl.ds(5 * WR + (NZ - 1) * BX + 8 * xt, 8), :] = zero
    first_rolls(0)
    bulk(0)
    for copy in loads[3]:
        copy.wait()
    for level in range(5):
        for half in range(2):
            receive(level, half)
            correct(level, half)
        if level < 4:
            bulk(level + 1, level - 1)
        sent(level)
    gram(3)

    for q in range(USED, LANES, 8):
        RED[pl.ds(q, 8), :] = zero
    total = lax.dot_general(
        jnp.ones((8, L), jnp.float32), RED[...], (((1,), (1,)), ((), ())),
        precision=lax.Precision.HIGHEST, preferred_element_type=jnp.float32,
    )

    def exchange(total, buffer, peers, send_sems, recv_sems):
        buffer[pl.ds(0, 8), :] = total
        copies = []
        for k, peer in enumerate(peers):
            copy = pltpu.make_async_remote_copy(
                src_ref=buffer.at[pl.ds(0, 2)], dst_ref=buffer.at[pl.ds(8 + 2 * k, 2)],
                send_sem=send_sems.at[k], recv_sem=recv_sems.at[k],
                device_id=peer, device_id_type=MESH,
            )
            copy.start()
            copies.append(copy)
        own = jnp.where(sub < 2, total, 0.0)
        for copy in copies:
            copy.wait_recv()
        parts = [own]
        for at in range(0, 2 * len(peers), 8):
            part = buffer[pl.ds(8 + at, 8), :]
            left = 2 * len(peers) - at
            parts.append(part if left >= 8 else jnp.where(sub < left, part, 0.0))
        while len(parts) > 1:
            parts = [
                parts[k] + parts[k + 1] if k + 1 < len(parts) else parts[k]
                for k in range(0, len(parts), 2)
            ]
        for copy in copies:
            copy.wait_send()
        total = parts[0]
        for d in (2, 4):
            total = total + pltpu.roll(total, d, 0)
        return total

    total = jnp.where((sub & 1) == 0, total[:, :L], total[:, L:])
    total = exchange(total, RA, inner_peers, sa, ra)
    total = exchange(total, RB, outer_peers, sb, rb)
    swapped = pltpu.roll(total, 1, 0)
    even_row = (sub & 1) == 0
    total = [jnp.where(even_row, total, swapped), jnp.where(even_row, swapped, total)]

    def entry(p):
        return jnp.broadcast_to(total[p // L][:, p % L : p % L + 1], (8, L))

    order = 16
    A = {}
    for i in range(order):
        for j in range(i + 1):
            A[i, j] = entry(TABLE[(i // R, i % R, j // R, j % R)])
    rhs = []
    for i in range(order):
        column = [entry(TABLE[(i // R, i % R, 4, r)]) for r in range(R)]
        rhs.append(
            jnp.where(sub == 0, column[0],
                      jnp.where(sub == 1, column[1],
                                jnp.where(sub == 2, column[2], column[3])))
        )
    lower, inverse = {}, []
    for k in range(order):
        inv = 1.0 / A[k, k]
        inverse.append(inv)
        for i in range(k + 1, order):
            lower[i, k] = A[i, k] * inv
        for i in range(k + 1, order):
            for j in range(k + 1, i + 1):
                A[i, j] = A[i, j] - lower[i, k] * A[j, k]
            rhs[i] = rhs[i] - lower[i, k] * rhs[k]
    coeffs = [None] * order
    for k in range(order - 1, -1, -1):
        value = rhs[k] * inverse[k]
        for i in range(order - 1, k, -1):
            value = value - lower[i, k] * coeffs[i]
        coeffs[k] = value
        for r in range(R):
            CS[pl.ds((r * order + k) * 8, 8), :] = jnp.broadcast_to(value[r : r + 1], (8, L))


UPDATE_STEPS = 8


def update(F, W, CS, sol_hbm, res_hbm, sol, res, sems):
    planes = NZ // UPDATE_STEPS

    def writes(step):
        where = (slice(None), pl.ds(step * planes, planes))
        return [
            pltpu.make_async_copy(source.at[where], target.at[where], sems.at[k, step])
            for k, (source, target) in enumerate(((sol, sol_hbm), (res, res_hbm)))
        ]

    def body(step, carry):
        def plane(k, carry):
            z = step * planes + k
            sums = []
            for r in range(R):
                for xt in range(XT):
                    row = pl.multiple_of((r * NZ + z) * BX + 8 * xt, 8)
                    sums.append([F[pl.ds(f * FS + PAD + row, 8), :] for f in range(2)])
            for i in range(16):
                coef = [CS[pl.ds((r * 16 + i) * 8, 8), :] for r in range(R)]
                for xt in range(XT):
                    row = pl.multiple_of(((i % R) * NZ + z) * BX + 8 * xt, 8)
                    basis = F[pl.ds((i // R + 1) * FS + PAD + row, 8), :]
                    image = W[pl.ds((i // R) * FR + row, 8), :]
                    for r in range(R):
                        both = sums[r * XT + xt]
                        both[0] = both[0] + coef[r] * basis
                        both[1] = both[1] - coef[r] * image
            for r in range(R):
                for xt in range(XT):
                    sol[r, z, pl.ds(8 * xt, 8), :] = sums[r * XT + xt][0]
                    res[r, z, pl.ds(8 * xt, 8), :] = sums[r * XT + xt][1]
            return carry

        lax.fori_loop(0, planes, plane, 0)
        for copy in writes(step):
            copy.start()
        return carry

    lax.fori_loop(0, UPDATE_STEPS, body, 0)
    for step in range(UPDATE_STEPS):
        for copy in writes(step):
            copy.wait()


def on_device(gx_size, gy_size, right_side, start_field, center, weights):
    inner = min(8, gx_size // 2)
    outer = gx_size // inner
    dma = pltpu.SemaphoreType.DMA
    f32 = jnp.float32
    flat = lambda a: a.reshape(-1, L)
    held = pltpu.MemorySpace.VMEM
    rows_for = lambda devices: 8 + (2 * devices + 5) // 8 * 8
    shape = lambda *dims: jax.ShapeDtypeStruct(dims, f32)
    in_hbm = lambda a: pltpu.with_memory_space_constraint(flat(a), pltpu.HBM)
    fields, images, coeffs = pl.pallas_call(
        functools.partial(kernel, gx_size, gy_size, inner),
        out_shape=[shape(5 * FS, L), shape(4 * FR, L), shape(64 * 8, L)],
        in_specs=[pl.BlockSpec(memory_space=pltpu.HBM)] * 4,
        out_specs=[pl.BlockSpec(memory_space=held)] * 3,
        scratch_shapes=[
            pltpu.VMEM((FR, L), f32),
            pltpu.VMEM((WR, L), f32),
            pltpu.VMEM((6 * WR, L), f32),
            pltpu.VMEM((WR, L), f32),
            pltpu.VMEM((2 * NZ * 8, L), f32),
            pltpu.VMEM((5, 2, 2, R * HALF, L), f32),
            pltpu.VMEM((5, 2, 2, BX, L), f32),
            pltpu.VMEM((5, 2, 2, R * HALF, L), f32),
            pltpu.VMEM((5, 2, BX, L), f32),
            pltpu.VMEM((2 * 2 * GROUP * R * XT * 8, L), f32),
            pltpu.VMEM((8 * USED, L), f32),
            pltpu.VMEM((LANES, L), f32),
            pltpu.VMEM((rows_for(inner), L), f32),
            pltpu.VMEM((rows_for(outer * gy_size), L), f32),
            dma((4, 6)),
            dma((5, 2, 2)), dma((5, 2, 2)), dma((5, 2, 2)), dma((5, 2, 2)),
            dma((inner,)), dma((inner,)),
            dma((outer * gy_size,)), dma((outer * gy_size,)),
        ],
        compiler_params=pltpu.CompilerParams(
            collective_id=0, has_side_effects=True, vmem_limit_bytes=32 * 1024 * 1024,
        ),
    )(in_hbm(right_side), in_hbm(start_field), in_hbm(center), in_hbm(weights))
    return pl.pallas_call(
        update,
        out_shape=[shape(R, NZ, BX, L)] * 2,
        in_specs=[pl.BlockSpec(memory_space=held)] * 3,
        out_specs=[pl.BlockSpec(memory_space=pltpu.HBM)] * 2,
        scratch_shapes=[pltpu.VMEM((R, NZ, BX, L), f32)] * 2 + [dma((2, UPDATE_STEPS))],
        compiler_params=pltpu.CompilerParams(vmem_limit_bytes=16 * 1024 * 1024),
    )(fields, images, coeffs)


def solution(mesh):
    gx_size, gy_size = mesh.shape["gx"], mesh.shape["gy"]
    return jax.shard_map(
        functools.partial(on_device, gx_size, gy_size),
        mesh=mesh,
        in_specs=(
            P(None, None, "gx", "gy"),
            P(None, None, "gx", "gy"),
            P(None, "gx", "gy"),
            P(None, None, "gx", "gy"),
        ),
        out_specs=(P(None, None, "gx", "gy"), P(None, None, "gx", "gy")),
        check_vma=False,
    )
```

```python
import functools

import jax
import jax.numpy as jnp
from jax import lax
from jax.experimental import pallas as pl
from jax.experimental.pallas import tpu as pltpu
from jax.sharding import PartitionSpec as P

SHIFTS = (12.0, 2.0, 8.0, 5.0)
SCALE_DOWN = 5.0
MESH = pl.DeviceIdType.MESH

R, NZ, BX, L = 4, 24, 24, 128
XT = BX // 8
FR = R * NZ * BX
WR = NZ * BX
PAD = 24
FS = FR + 2 * PAD
HALF = NZ // 2
GROUP = 4
STEPS = NZ // GROUP


def pair_table():
    table, groups, at = {}, [], 0
    for level in range(4):
        for other in (level, 4) + tuple(range(level)):
            pairs = [
                (a, b)
                for a in range(R)
                for b in range(R)
                if other != level or b <= a
            ]
            for index, (a, b) in enumerate(pairs):
                table[(level, a, other, b)] = at + index
            groups.append((level, other, at, pairs))
            at += (len(pairs) + 7) // 8 * 8
    return table, groups, at


TABLE, GROUPS, USED = pair_table()
LANES = 256


def kernel(
    gx_size, gy_size, inner,
    b_hbm, x0_hbm, c_hbm, w_hbm,
    F, W, CS,
    B, C6, WM, WE, WX, HX, HY, XS, YS, RING, ACC, RED, RA, RB,
    ld, sx, rx, sy, ry, sa, ra, sb, rb,
):
    gx = lax.axis_index("gx")
    gy = lax.axis_index("gy")
    outer = gx_size // inner
    base_x = (gx // inner) * inner
    in_x = gx - base_x

    loads = [[], [], [], []]
    for group, (source, ref, offset, parts) in enumerate((
        (x0_hbm, F, PAD, R), (w_hbm, WM, 0, 6), (c_hbm, C6, 0, 1), (b_hbm, B, 0, R),
    )):
        rows = source.shape[0] // parts
        for part in range(parts):
            copy = pltpu.make_async_copy(
                source.at[pl.ds(part * rows, rows)],
                ref.at[pl.ds(offset + part * rows, rows)],
                ld.at[group, part],
            )
            loads[group].append(copy)
    for copy in loads[0] + loads[2] + loads[1]:
        copy.start()

    barrier = pltpu.get_barrier_semaphore()
    hello = []
    for step in (1, gx_size - 1):
        hello.append((lax.rem(gx + step, gx_size), gy))
    for step in (1, gy_size - 1):
        hello.append((gx, lax.rem(gy + step, gy_size)))
    far = lambda step, size: -min(step, size - step)
    inner_steps = sorted(range(1, inner), key=lambda i: far(i, inner))
    inner_peers = [(base_x + lax.rem(in_x + i, inner), gy) for i in inner_steps]
    outer_peers = []
    outer_steps = [(i, j) for i in range(outer) for j in range(gy_size) if i or j]
    outer_steps.sort(key=lambda s: far(s[0], outer) + far(s[1], gy_size))
    for i, j in outer_steps:
        outer_peers.append((lax.rem(gx + i * inner, gx_size), lax.rem(gy + j, gy_size)))
    for peer in hello + inner_peers + outer_peers:
        pl.semaphore_signal(barrier, inc=1, device_id=peer, device_id_type=MESH)

    zero = jnp.zeros((8, L), jnp.float32)
    lane = lax.broadcasted_iota(jnp.int32, (8, L), 1)
    sub = lax.broadcasted_iota(jnp.int32, (8, L), 0)
    first_x, last_x = gx == 0, gx == gx_size - 1
    first_y, last_y = gy == 0, gy == gy_size - 1
    for f in range(5):
        for p in range(3):
            F[pl.ds(f * FS + 8 * p, 8), :] = zero
            F[pl.ds(f * FS + PAD + FR + 8 * p, 8), :] = zero

    for cond, ref, side in (
        (first_x, HX, 0), (last_x, HX, 1), (first_y, HY, 0), (last_y, HY, 1),
    ):
        @pl.when(cond)
        def _(ref=ref, side=side):
            for level in range(5):
                for half in range(2):
                    for q in range(ref.shape[3] // 8):
                        ref[level, half, side, pl.ds(8 * q, 8), :] = zero

    tiles = [(xt, r) for xt in range(XT) for r in range(R)]

    def tile_row(r, z, xt):
        return (r * NZ + z) * BX + 8 * xt

    def aligned(row):
        return row if isinstance(row, int) else pl.multiple_of(row, 8)

    def pack_lane(r, zh):
        return 2 * (r * HALF + zh)

    def pack_tile(tile, r, zh, acc):
        j2 = pack_lane(r, zh)
        mask = ((lane + (1 - j2)) & (L - 1)) < 2
        return jnp.where(mask, pltpu.roll(tile, j2, 1), acc)

    up_x, down_x = (lax.rem(gx + 1, gx_size), gy), (lax.rem(gx + gx_size - 1, gx_size), gy)
    up_y, down_y = (gx, lax.rem(gy + 1, gy_size)), (gx, lax.rem(gy + gy_size - 1, gy_size))

    def copies_x(level, half):
        return [
            pltpu.make_async_remote_copy(
                src_ref=XS.at[level, half, 1 - lands], dst_ref=HX.at[level, half, lands],
                send_sem=sx.at[level, half, lands], recv_sem=rx.at[level, half, lands],
                device_id=peer, device_id_type=MESH)
            for lands, peer in enumerate((up_x, down_x))
        ]

    def copies_y(level, half):
        return [
            pltpu.make_async_remote_copy(
                src_ref=YS.at[level, half], dst_ref=HY.at[level, half, lands],
                send_sem=sy.at[level, half, lands], recv_sem=ry.at[level, half, lands],
                device_id=peer, device_id_type=MESH)
            for lands, peer in enumerate((up_y, down_y))
        ]

    def send_x(level, half):
        for missing, copy in zip((last_x, first_x), copies_x(level, half)):
            @pl.when(jnp.logical_not(missing))
            def _(copy=copy):
                copy.start()

    def send_y(level, half, acc):
        for xt in range(XT):
            YS[level, half, pl.ds(8 * xt, 8), :] = acc[xt]
        for missing, copy in zip((last_y, first_y), copies_y(level, half)):
            @pl.when(jnp.logical_not(missing))
            def _(copy=copy):
                copy.start()

    def receive_x(level, half):
        for missing, copy in zip((first_x, last_x), copies_x(level, half)):
            @pl.when(jnp.logical_not(missing))
            def _(copy=copy):
                copy.wait_recv()

    def receive_y(level, half):
        for missing, copy in zip((first_y, last_y), copies_y(level, half)):
            @pl.when(jnp.logical_not(missing))
            def _(copy=copy):
                copy.wait_recv()

    def sent(level):
        for half in range(2):
            for missing, copy in zip(
                (last_x, first_x, last_y, first_y), copies_x(level, half) + copies_y(level, half)
            ):
                @pl.when(jnp.logical_not(missing))
                def _(copy=copy):
                    copy.wait_send()

    slot = 2 * GROUP * R * XT * 8

    def keep_rolls(level, z0, at):
            base = level * FS + PAD
            kept = []
            for k in range(GROUP):
                for index, (xt, r) in enumerate(tiles):
                    mid = F[pl.ds(aligned(base + tile_row(r, z0 + k, xt)), 8), :]
                    where = at + 16 * (k * R * XT + index)
                    kept.append((where, pltpu.roll(mid, 1, 1)))
                    kept.append((where + 8, pltpu.roll(mid, L - 1, 1)))
            return kept

    def first_rolls(level):
        for at, value in keep_rolls(level, 0, 0):
            RING[pl.ds(at, 8), :] = value

    def rows_of(block, r, z, xt):
        row = aligned(tile_row(r, z, xt))
        if block == 4:
            return F[pl.ds(FS + PAD + row, 8), :]
        return W[pl.ds(block * FR + row, 8), :]

    def products(lev, other, pairs, places, acc):
        for z, xt in places:
            left = [rows_of(lev, r, z, xt) for r in range(R)]
            right = left if other == lev else [rows_of(other, r, z, xt) for r in range(R)]
            for index, (a, b) in enumerate(pairs):
                acc[index] = acc[index] + left[a] * right[b]

    def fold(sums, start):
        sums = sums + [zero] * (-len(sums) % 8)
        for q in range(0, len(sums), 8):
            part = sums[q : q + 8]
            for d in (1, 2, 4):
                part = [combine(part[k], part[k + 1], d) for k in range(0, len(part), 2)]
            RED[pl.ds(start + q, 8), :] = part[0]

    def bulk(level, gram_level=None):
        base = level * FS + PAD
        out = max(level - 1, 0) * FR
        groups = [g for g in GROUPS if g[0] == gram_level]
        for _, _, start, pairs in groups:
            for index in range(len(pairs)):
                ACC[pl.ds(8 * (start + index), 8), :] = zero

        def body(step, carry):
            now = pl.multiple_of(lax.rem(step, 2) * slot, 8)
            later = pl.multiple_of(slot - now, 8)
            kept = keep_rolls(level, jnp.minimum(step + 1, STEPS - 1) * GROUP, later)
            stores = []
            for k in range(GROUP):
                z = step * GROUP + k
                for xt in range(XT):
                    wrow = pl.multiple_of(z * BX + 8 * xt, 8)
                    w = [WM[pl.ds(i * WR + wrow, 8), :] for i in range(6)]
                    c6 = C6[pl.ds(wrow, 8), :]
                    for r in range(R):
                        ring = now + 16 * ((k * XT + xt) * R + r)
                        row = pl.multiple_of(tile_row(r, z, xt), 8)
                        at = base + row
                        low = RING[pl.ds(ring, 8), :]
                        high = RING[pl.ds(ring + 8, 8), :]
                        beside = w[0] * F[pl.ds(at - 1, 8), :] + w[1] * F[pl.ds(at + 1, 8), :]
                        beside = beside + (w[2] * low + w[3] * high)
                        beside = beside + (
                            w[4] * F[pl.ds(at - BX, 8), :] + w[5] * F[pl.ds(at + BX, 8), :]
                        )
                        stores.append((out + row, c6 * F[pl.ds(at, 8), :] - beside))
            places = [(step * GROUP + k, xt) for k in range(GROUP) for xt in range(XT)]
            for lev, other, start, pairs in groups:
                where = [pl.ds(8 * (start + index), 8) for index in range(len(pairs))]
                acc = [ACC[w, :] for w in where]
                products(lev, other, pairs, places, acc)
                for w, value in zip(where, acc):
                    ACC[w, :] = value
            for at, value in stores:
                W[pl.ds(at, 8), :] = value
            for at, value in kept:
                RING[pl.ds(at, 8), :] = value
            return carry

        lax.fori_loop(0, STEPS, body, 0)
        for _, _, start, pairs in groups:
            fold([ACC[pl.ds(8 * (start + index), 8), :] for index in range(len(pairs))], start)

    def correct(level, half):
        out = max(level - 1, 0) * FR
        ahead = (level + 1) * FS + PAD
        receive_y(level, half)
        even = (lane & 1) == 0
        halos = [
            jnp.where(
                even,
                pltpu.roll(HY[level, half, 0, pl.ds(8 * xt, 8), :], 1, 1),
                pltpu.roll(HY[level, half, 1, pl.ds(8 * xt, 8), :], L - 1, 1),
            )
            for xt in range(XT)
        ]
        def columns(zh, xt, r):
            z = half * HALF + zh
            halo = pltpu.roll(halos[xt], (L - pack_lane(r, zh)) % L, 1)
            edge = WE[pl.ds(z * BX + 8 * xt, 8), :]
            return W[pl.ds(out + tile_row(r, z, xt), 8), :] - edge * halo

        def finish(zh, xt, r, image):
            row = tile_row(r, half * HALF + zh, xt)
            if level == 0:
                following = B[pl.ds(row, 8), :] - image
            else:
                W[pl.ds(out + row, 8), :] = image
                held = F[pl.ds(level * FS + PAD + row, 8), :]
                following = image * (1.0 / SCALE_DOWN) - held * (
                    SHIFTS[level - 1] / SCALE_DOWN
                )
            if level < 4:
                F[pl.ds(ahead + row, 8), :] = following
            return following

        for zh in range(HALF):
            for xt in (0, XT - 1):
                for r in range(R):
                    row = tile_row(r, half * HALF + zh, xt)
                    W[pl.ds(out + row, 8), :] = columns(zh, xt, r)
        for zh in range(HALF):
            for xt in range(1, XT - 1):
                for r in range(R):
                    finish(zh, xt, r, columns(zh, xt, r))
        receive_x(level, half)
        for zh in range(HALF):
            z = half * HALF + zh
            for side, xt, take in ((0, 0, 0), (1, XT - 1, 7)):
                edge = WX[pl.ds((side * NZ + z) * 8, 8), :]
                for r in range(R):
                    halo = HX[level, half, side, pl.ds(r * HALF + zh, 1), :]
                    image = W[pl.ds(out + tile_row(r, z, xt), 8), :]
                    image = image - edge * jnp.broadcast_to(halo, (8, L))
                    following = finish(zh, xt, r, image)
                    if level < 4:
                        XS[level + 1, half, side, pl.ds(r * HALF + zh, 1), :] = (
                            following[take : take + 1]
                        )
        if level < 4:
            send_x(level + 1, half)
        if level < 4:
            acc = [zero] * XT
            for zh in range(HALF):
                for xt, r in tiles:
                    row = tile_row(r, half * HALF + zh, xt)
                    acc[xt] = pack_tile(F[pl.ds(ahead + row, 8), :], r, zh, acc[xt])
            send_y(level + 1, half, acc)
        if half and level < 4:
            first_rolls(level + 1)

    def combine(a, b, d):
        mask = (sub & d) == 0
        return jnp.where(mask, a, b) + pltpu.roll(jnp.where(mask, b, a), d, 0)

    def gram(level):
        for lev, other, start, pairs in GROUPS:
            if lev != level:
                continue

            def body(step, acc):
                acc = list(acc)
                places = [(2 * step + k, xt) for k in range(2) for xt in range(XT)]
                products(lev, other, pairs, places, acc)
                return tuple(acc)

            fold(list(lax.fori_loop(0, NZ // 2, body, (zero,) * len(pairs))), start)

    for copy in loads[0]:
        copy.wait()
    for copy in loads[3]:
        copy.start()

    packed = []
    for half in range(2):
        def pack_body(step, acc, half=half):
            acc = list(acc)
            for k in range(GROUP):
                zh = step * GROUP + k
                for xt, r in tiles:
                    row = pl.multiple_of(PAD + tile_row(r, half * HALF + zh, xt), 8)
                    tile = F[pl.ds(row, 8), :]
                    acc[xt] = pack_tile(tile, r, zh, acc[xt])
                    for side, where, take in ((0, 0, 0), (1, XT - 1, 7)):
                        if xt == where:
                            XS[0, half, side, pl.ds(r * HALF + zh, 1), :] = tile[take : take + 1]
            return tuple(acc)

        packed.append(lax.fori_loop(0, HALF // GROUP, pack_body, (zero,) * XT))
    pl.semaphore_wait(barrier, len(hello) + len(inner_peers) + len(outer_peers))
    for half in range(2):
        send_x(0, half)
        send_y(0, half, packed[half])

    for copy in loads[1] + loads[2]:
        copy.wait()

    def prepare(z, carry):
        stores = []
        for xt in range(XT):
            row = pl.multiple_of(z * BX + 8 * xt, 8)
            stores.append((C6, row, C6[pl.ds(row, 8), :] + 6.0))
            for side, where, inside, ends in (
                (0, 0, sub != 0, first_x), (1, XT - 1, sub != 7, last_x)
            ):
                if xt == where:
                    w = WM[pl.ds(side * WR + row, 8), :]
                    stores.append((WM, side * WR + row, jnp.where(inside, w, 0.0)))
                    at = pl.multiple_of((side * NZ + z) * 8, 8)
                    stores.append((WX, at, jnp.where(inside | ends, 0.0, w)))
            low = WM[pl.ds(2 * WR + row, 8), :]
            high = WM[pl.ds(3 * WR + row, 8), :]
            edge = jnp.where((lane == 0) & jnp.logical_not(first_y), low, 0.0)
            edge = jnp.where((lane == L - 1) & jnp.logical_not(last_y), high, edge)
            stores.append((WE, row, edge))
            stores.append((WM, 2 * WR + row, jnp.where(lane == 0, 0.0, low)))
            stores.append((WM, 3 * WR + row, jnp.where(lane == L - 1, 0.0, high)))
        for ref, at, value in stores:
            ref[pl.ds(at, 8), :] = value
        return carry

    lax.fori_loop(0, NZ, prepare, 0)
    for xt in range(XT):
        WM[pl.ds(4 * WR + 8 * xt, 8), :] = zero
        WM[pl.ds(5 * WR + (NZ - 1) * BX + 8 * xt, 8), :] = zero
    first_rolls(0)
    bulk(0)
    for copy in loads[3]:
        copy.wait()
    for level in range(5):
        for half in range(2):
            correct(level, half)
        if level < 4:
            bulk(level + 1, level - 1)
        sent(level)
    gram(3)

    for q in range(USED, LANES, 8):
        RED[pl.ds(q, 8), :] = zero
    total = lax.dot_general(
        jnp.ones((8, L), jnp.float32), RED[...], (((1,), (1,)), ((), ())),
        precision=lax.Precision.HIGHEST, preferred_element_type=jnp.float32,
    )

    pending = []

    def exchange(total, buffer, peers, send_sems, recv_sems):
        buffer[pl.ds(0, 8), :] = total
        copies = []
        for k, peer in enumerate(peers):
            copy = pltpu.make_async_remote_copy(
                src_ref=buffer.at[pl.ds(0, 2)], dst_ref=buffer.at[pl.ds(8 + 2 * k, 2)],
                send_sem=send_sems.at[k], recv_sem=recv_sems.at[k],
                device_id=peer, device_id_type=MESH,
            )
            copy.start()
            copies.append(copy)
        own = jnp.where(sub < 2, total, 0.0)
        for copy in copies:
            copy.wait_recv()
        parts = [own]
        for at in range(0, 2 * len(peers), 8):
            part = buffer[pl.ds(8 + at, 8), :]
            left = 2 * len(peers) - at
            parts.append(part if left >= 8 else jnp.where(sub < left, part, 0.0))
        while len(parts) > 1:
            parts = [
                parts[k] + parts[k + 1] if k + 1 < len(parts) else parts[k]
                for k in range(0, len(parts), 2)
            ]
        pending.extend(copies)
        total = parts[0]
        for d in (2, 4):
            total = total + pltpu.roll(total, d, 0)
        return total

    total = jnp.where((sub & 1) == 0, total[:, :L], total[:, L:])
    total = exchange(total, RA, inner_peers, sa, ra)
    total = exchange(total, RB, outer_peers, sb, rb)
    swapped = pltpu.roll(total, 1, 0)
    even_row = (sub & 1) == 0
    total = [jnp.where(even_row, total, swapped), jnp.where(even_row, swapped, total)]

    def entry(p):
        return jnp.broadcast_to(total[p // L][:, p % L : p % L + 1], (8, L))

    order = 16
    A = {}
    for i in range(order):
        for j in range(i + 1):
            A[i, j] = entry(TABLE[(i // R, i % R, j // R, j % R)])
    rhs = []
    for i in range(order):
        column = [entry(TABLE[(i // R, i % R, 4, r)]) for r in range(R)]
        rhs.append(
            jnp.where(sub == 0, column[0],
                      jnp.where(sub == 1, column[1],
                                jnp.where(sub == 2, column[2], column[3])))
        )
    lower, inverse = {}, []
    for k in range(order):
        inv = 1.0 / A[k, k]
        inverse.append(inv)
        for i in range(k + 1, order):
            lower[i, k] = A[i, k] * inv
        for i in range(k + 1, order):
            for j in range(k + 1, i + 1):
                A[i, j] = A[i, j] - lower[i, k] * A[j, k]
            rhs[i] = rhs[i] - lower[i, k] * rhs[k]
    coeffs = [None] * order
    for k in range(order - 1, -1, -1):
        value = rhs[k] * inverse[k]
        for i in range(order - 1, k, -1):
            value = value - lower[i, k] * coeffs[i]
        coeffs[k] = value
        for r in range(R):
            CS[pl.ds((r * order + k) * 8, 8), :] = jnp.broadcast_to(value[r : r + 1], (8, L))
    for copy in pending:
        copy.wait_send()


UPDATE_STEPS = 8


def update(F, W, CS, sol_hbm, res_hbm, sol, res, sems):
    planes = NZ // UPDATE_STEPS

    def writes(step):
        where = (slice(None), pl.ds(step * planes, planes))
        return [
            pltpu.make_async_copy(source.at[where], target.at[where], sems.at[k, step])
            for k, (source, target) in enumerate(((sol, sol_hbm), (res, res_hbm)))
        ]

    def body(step, carry):
        def plane(k, carry):
            z = step * planes + k
            sums = []
            for r in range(R):
                for xt in range(XT):
                    row = pl.multiple_of((r * NZ + z) * BX + 8 * xt, 8)
                    sums.append([F[pl.ds(f * FS + PAD + row, 8), :] for f in range(2)])
            for i in range(16):
                coef = [CS[pl.ds((r * 16 + i) * 8, 8), :] for r in range(R)]
                for xt in range(XT):
                    row = pl.multiple_of(((i % R) * NZ + z) * BX + 8 * xt, 8)
                    basis = F[pl.ds((i // R + 1) * FS + PAD + row, 8), :]
                    image = W[pl.ds((i // R) * FR + row, 8), :]
                    for r in range(R):
                        both = sums[r * XT + xt]
                        both[0] = both[0] + coef[r] * basis
                        both[1] = both[1] - coef[r] * image
            for r in range(R):
                for xt in range(XT):
                    sol[r, z, pl.ds(8 * xt, 8), :] = sums[r * XT + xt][0]
                    res[r, z, pl.ds(8 * xt, 8), :] = sums[r * XT + xt][1]
            return carry

        lax.fori_loop(0, planes, plane, 0)
        for copy in writes(step):
            copy.start()
        return carry

    lax.fori_loop(0, UPDATE_STEPS, body, 0)
    for step in range(UPDATE_STEPS):
        for copy in writes(step):
            copy.wait()


def on_device(gx_size, gy_size, right_side, start_field, center, weights):
    inner = min(8, gx_size // 2)
    outer = gx_size // inner
    dma = pltpu.SemaphoreType.DMA
    f32 = jnp.float32
    flat = lambda a: a.reshape(-1, L)
    held = pltpu.MemorySpace.VMEM
    rows_for = lambda devices: 8 + (2 * devices + 5) // 8 * 8
    shape = lambda *dims: jax.ShapeDtypeStruct(dims, f32)
    in_hbm = lambda a: pltpu.with_memory_space_constraint(flat(a), pltpu.HBM)
    fields, images, coeffs = pl.pallas_call(
        functools.partial(kernel, gx_size, gy_size, inner),
        out_shape=[shape(5 * FS, L), shape(4 * FR, L), shape(64 * 8, L)],
        in_specs=[pl.BlockSpec(memory_space=pltpu.HBM)] * 4,
        out_specs=[pl.BlockSpec(memory_space=held)] * 3,
        scratch_shapes=[
            pltpu.VMEM((FR, L), f32),
            pltpu.VMEM((WR, L), f32),
            pltpu.VMEM((6 * WR, L), f32),
            pltpu.VMEM((WR, L), f32),
            pltpu.VMEM((2 * NZ * 8, L), f32),
            pltpu.VMEM((5, 2, 2, R * HALF, L), f32),
            pltpu.VMEM((5, 2, 2, BX, L), f32),
            pltpu.VMEM((5, 2, 2, R * HALF, L), f32),
            pltpu.VMEM((5, 2, BX, L), f32),
            pltpu.VMEM((2 * 2 * GROUP * R * XT * 8, L), f32),
            pltpu.VMEM((8 * USED, L), f32),
            pltpu.VMEM((LANES, L), f32),
            pltpu.VMEM((rows_for(inner), L), f32),
            pltpu.VMEM((rows_for(outer * gy_size), L), f32),
            dma((4, 6)),
            dma((5, 2, 2)), dma((5, 2, 2)), dma((5, 2, 2)), dma((5, 2, 2)),
            dma((inner,)), dma((inner,)),
            dma((outer * gy_size,)), dma((outer * gy_size,)),
        ],
        compiler_params=pltpu.CompilerParams(
            collective_id=0, has_side_effects=True, vmem_limit_bytes=32 * 1024 * 1024,
        ),
    )(in_hbm(right_side), in_hbm(start_field), in_hbm(center), in_hbm(weights))
    return pl.pallas_call(
        update,
        out_shape=[shape(R, NZ, BX, L)] * 2,
        in_specs=[pl.BlockSpec(memory_space=held)] * 3,
        out_specs=[pl.BlockSpec(memory_space=pltpu.HBM)] * 2,
        scratch_shapes=[pltpu.VMEM((R, NZ, BX, L), f32)] * 2 + [dma((2, UPDATE_STEPS))],
        compiler_params=pltpu.CompilerParams(vmem_limit_bytes=16 * 1024 * 1024),
    )(fields, images, coeffs)


def solution(mesh):
    gx_size, gy_size = mesh.shape["gx"], mesh.shape["gy"]
    return jax.shard_map(
        functools.partial(on_device, gx_size, gy_size),
        mesh=mesh,
        in_specs=(
            P(None, None, "gx", "gy"),
            P(None, None, "gx", "gy"),
            P(None, "gx", "gy"),
            P(None, None, "gx", "gy"),
        ),
        out_specs=(P(None, None, "gx", "gy"), P(None, None, "gx", "gy")),
        check_vma=False,
    )
```

```python
import functools

import jax
import jax.numpy as jnp
from jax import lax
from jax.experimental import pallas as pl
from jax.experimental.pallas import tpu as pltpu
from jax.sharding import PartitionSpec as P

SHIFTS = (12.0, 2.0, 8.0, 5.0)
SCALE_DOWN = 5.0
MESH = pl.DeviceIdType.MESH

R, NZ, BX, L = 4, 24, 24, 128
XT = BX // 8
FR = R * NZ * BX
WR = NZ * BX
PAD = 24
FS = FR + 2 * PAD
HALF = NZ // 2
GROUP = 4
STEPS = NZ // GROUP


def pair_table():
    table, groups, at = {}, [], 0
    for level in range(4):
        for other in (level, 4) + tuple(range(level)):
            pairs = [
                (a, b)
                for a in range(R)
                for b in range(R)
                if other != level or b <= a
            ]
            for index, (a, b) in enumerate(pairs):
                table[(level, a, other, b)] = at + index
            groups.append((level, other, at, pairs))
            at += (len(pairs) + 7) // 8 * 8
    return table, groups, at


TABLE, GROUPS, USED = pair_table()
LANES = 256


def kernel(
    gx_size, gy_size, inner,
    b_hbm, x0_hbm, c_hbm, w_hbm,
    F, W, CS,
    B, C6, WM, WE, WX, HX, HY, XS, YS, RING, ACC, RED, RA, RB,
    ld, sx, rx, sy, ry, sa, ra, sb, rb,
):
    gx = lax.axis_index("gx")
    gy = lax.axis_index("gy")
    outer = gx_size // inner
    base_x = (gx // inner) * inner
    in_x = gx - base_x

    loads = [[], [], [], []]
    for group, (source, ref, offset, parts) in enumerate((
        (x0_hbm, F, PAD, R), (w_hbm, WM, 0, 6), (c_hbm, C6, 0, 1), (b_hbm, B, 0, R),
    )):
        rows = source.shape[0] // parts
        for part in range(parts):
            copy = pltpu.make_async_copy(
                source.at[pl.ds(part * rows, rows)],
                ref.at[pl.ds(offset + part * rows, rows)],
                ld.at[group, part],
            )
            loads[group].append(copy)
    for copy in loads[0] + loads[2] + loads[1]:
        copy.start()

    barrier = pltpu.get_barrier_semaphore()
    hello = []
    for step in (1, gx_size - 1):
        hello.append((lax.rem(gx + step, gx_size), gy))
    for step in (1, gy_size - 1):
        hello.append((gx, lax.rem(gy + step, gy_size)))
    far = lambda step, size: -min(step, size - step)
    inner_steps = sorted(range(1, inner), key=lambda i: far(i, inner))
    inner_peers = [(base_x + lax.rem(in_x + i, inner), gy) for i in inner_steps]
    outer_peers = []
    outer_steps = [(i, j) for i in range(outer) for j in range(gy_size) if i or j]
    outer_steps.sort(key=lambda s: far(s[0], outer) + far(s[1], gy_size))
    for i, j in outer_steps:
        outer_peers.append((lax.rem(gx + i * inner, gx_size), lax.rem(gy + j, gy_size)))
    for peer in hello + inner_peers + outer_peers:
        pl.semaphore_signal(barrier, inc=1, device_id=peer, device_id_type=MESH)

    zero = jnp.zeros((8, L), jnp.float32)
    lane = lax.broadcasted_iota(jnp.int32, (8, L), 1)
    sub = lax.broadcasted_iota(jnp.int32, (8, L), 0)
    first_x, last_x = gx == 0, gx == gx_size - 1
    first_y, last_y = gy == 0, gy == gy_size - 1
    for f in range(5):
        for p in range(3):
            F[pl.ds(f * FS + 8 * p, 8), :] = zero
            F[pl.ds(f * FS + PAD + FR + 8 * p, 8), :] = zero

    for cond, ref, side in (
        (first_x, HX, 0), (last_x, HX, 1), (first_y, HY, 0), (last_y, HY, 1),
    ):
        @pl.when(cond)
        def _(ref=ref, side=side):
            for level in range(5):
                for half in range(2):
                    for q in range(ref.shape[3] // 8):
                        ref[level, half, side, pl.ds(8 * q, 8), :] = zero

    tiles = [(xt, r) for xt in range(XT) for r in range(R)]

    def tile_row(r, z, xt):
        return (r * NZ + z) * BX + 8 * xt

    def aligned(row):
        return row if isinstance(row, int) else pl.multiple_of(row, 8)

    def pack_lane(r, zh):
        return 2 * (r * HALF + zh)

    def pack_tile(tile, r, zh, acc):
        j2 = pack_lane(r, zh)
        mask = ((lane + (1 - j2)) & (L - 1)) < 2
        return jnp.where(mask, pltpu.roll(tile, j2, 1), acc)

    up_x, down_x = (lax.rem(gx + 1, gx_size), gy), (lax.rem(gx + gx_size - 1, gx_size), gy)
    up_y, down_y = (gx, lax.rem(gy + 1, gy_size)), (gx, lax.rem(gy + gy_size - 1, gy_size))

    def copies_x(level, half):
        return [
            pltpu.make_async_remote_copy(
                src_ref=XS.at[level, half, 1 - lands], dst_ref=HX.at[level, half, lands],
                send_sem=sx.at[level, half, lands], recv_sem=rx.at[level, half, lands],
                device_id=peer, device_id_type=MESH)
            for lands, peer in enumerate((up_x, down_x))
        ]

    def copies_y(level, half):
        return [
            pltpu.make_async_remote_copy(
                src_ref=YS.at[level, half], dst_ref=HY.at[level, half, lands],
                send_sem=sy.at[level, half, lands], recv_sem=ry.at[level, half, lands],
                device_id=peer, device_id_type=MESH)
            for lands, peer in enumerate((up_y, down_y))
        ]

    def send_x(level, half):
        for missing, copy in zip((last_x, first_x), copies_x(level, half)):
            @pl.when(jnp.logical_not(missing))
            def _(copy=copy):
                copy.start()

    def send_y(level, half, acc):
        for xt in range(XT):
            YS[level, half, pl.ds(8 * xt, 8), :] = acc[xt]
        for missing, copy in zip((last_y, first_y), copies_y(level, half)):
            @pl.when(jnp.logical_not(missing))
            def _(copy=copy):
                copy.start()

    def receive_x(level, half):
        for missing, copy in zip((first_x, last_x), copies_x(level, half)):
            @pl.when(jnp.logical_not(missing))
            def _(copy=copy):
                copy.wait_recv()

    def receive_y(level, half):
        for missing, copy in zip((first_y, last_y), copies_y(level, half)):
            @pl.when(jnp.logical_not(missing))
            def _(copy=copy):
                copy.wait_recv()

    def sent(level):
        for half in range(2):
            for missing, copy in zip(
                (last_x, first_x, last_y, first_y), copies_x(level, half) + copies_y(level, half)
            ):
                @pl.when(jnp.logical_not(missing))
                def _(copy=copy):
                    copy.wait_send()

    slot = 2 * GROUP * R * XT * 8

    def keep_rolls(level, z0, at):
            base = level * FS + PAD
            kept = []
            for k in range(GROUP):
                for index, (xt, r) in enumerate(tiles):
                    mid = F[pl.ds(aligned(base + tile_row(r, z0 + k, xt)), 8), :]
                    where = at + 16 * (k * R * XT + index)
                    kept.append((where, pltpu.roll(mid, 1, 1)))
                    kept.append((where + 8, pltpu.roll(mid, L - 1, 1)))
            return kept

    def first_rolls(level):
        for at, value in keep_rolls(level, 0, 0):
            RING[pl.ds(at, 8), :] = value

    def rows_of(block, r, z, xt):
        row = aligned(tile_row(r, z, xt))
        if block == 4:
            return F[pl.ds(FS + PAD + row, 8), :]
        return W[pl.ds(block * FR + row, 8), :]

    def products(lev, other, pairs, places, acc):
        for z, xt in places:
            left = [rows_of(lev, r, z, xt) for r in range(R)]
            right = left if other == lev else [rows_of(other, r, z, xt) for r in range(R)]
            for index, (a, b) in enumerate(pairs):
                acc[index] = acc[index] + left[a] * right[b]

    def fold(sums, start):
        sums = sums + [zero] * (-len(sums) % 8)
        for q in range(0, len(sums), 8):
            part = sums[q : q + 8]
            for d in (1, 2, 4):
                part = [combine(part[k], part[k + 1], d) for k in range(0, len(part), 2)]
            RED[pl.ds(start + q, 8), :] = part[0]

    def bulk(level, gram_level=None):
        base = level * FS + PAD
        out = max(level - 1, 0) * FR
        groups = [g for g in GROUPS if g[0] == gram_level]
        for _, _, start, pairs in groups:
            for index in range(len(pairs)):
                ACC[pl.ds(8 * (start + index), 8), :] = zero

        def body(step, carry):
            now = pl.multiple_of(lax.rem(step, 2) * slot, 8)
            later = pl.multiple_of(slot - now, 8)
            kept = keep_rolls(level, jnp.minimum(step + 1, STEPS - 1) * GROUP, later)
            stores = []
            for k in range(GROUP):
                z = step * GROUP + k
                for xt in range(XT):
                    wrow = pl.multiple_of(z * BX + 8 * xt, 8)
                    w = [WM[pl.ds(i * WR + wrow, 8), :] for i in range(6)]
                    c6 = C6[pl.ds(wrow, 8), :]
                    for r in range(R):
                        ring = now + 16 * ((k * XT + xt) * R + r)
                        row = pl.multiple_of(tile_row(r, z, xt), 8)
                        at = base + row
                        low = RING[pl.ds(ring, 8), :]
                        high = RING[pl.ds(ring + 8, 8), :]
                        beside = w[0] * F[pl.ds(at - 1, 8), :] + w[1] * F[pl.ds(at + 1, 8), :]
                        beside = beside + (w[2] * low + w[3] * high)
                        beside = beside + (
                            w[4] * F[pl.ds(at - BX, 8), :] + w[5] * F[pl.ds(at + BX, 8), :]
                        )
                        stores.append((out + row, c6 * F[pl.ds(at, 8), :] - beside))
            places = [(step * GROUP + k, xt) for k in range(GROUP) for xt in range(XT)]
            for lev, other, start, pairs in groups:
                where = [pl.ds(8 * (start + index), 8) for index in range(len(pairs))]
                acc = [ACC[w, :] for w in where]
                products(lev, other, pairs, places, acc)
                for w, value in zip(where, acc):
                    ACC[w, :] = value
            for at, value in stores:
                W[pl.ds(at, 8), :] = value
            for at, value in kept:
                RING[pl.ds(at, 8), :] = value
            return carry

        lax.fori_loop(0, STEPS, body, 0)
        for _, _, start, pairs in groups:
            fold([ACC[pl.ds(8 * (start + index), 8), :] for index in range(len(pairs))], start)

    def correct(level, half):
        out = max(level - 1, 0) * FR
        ahead = (level + 1) * FS + PAD
        receive_y(level, half)
        even = (lane & 1) == 0
        halos = [
            jnp.where(
                even,
                pltpu.roll(HY[level, half, 0, pl.ds(8 * xt, 8), :], 1, 1),
                pltpu.roll(HY[level, half, 1, pl.ds(8 * xt, 8), :], L - 1, 1),
            )
            for xt in range(XT)
        ]
        def columns(zh, xt, r):
            z = half * HALF + zh
            halo = pltpu.roll(halos[xt], (L - pack_lane(r, zh)) % L, 1)
            edge = WE[pl.ds(z * BX + 8 * xt, 8), :]
            return W[pl.ds(out + tile_row(r, z, xt), 8), :] - edge * halo

        def finish(zh, xt, r, image):
            row = tile_row(r, half * HALF + zh, xt)
            if level == 0:
                following = B[pl.ds(row, 8), :] - image
            else:
                W[pl.ds(out + row, 8), :] = image
                held = F[pl.ds(level * FS + PAD + row, 8), :]
                following = image * (1.0 / SCALE_DOWN) - held * (
                    SHIFTS[level - 1] / SCALE_DOWN
                )
            if level < 4:
                F[pl.ds(ahead + row, 8), :] = following
            return following

        acc = [zero] * XT
        for zh in range(HALF):
            for xt in (0, XT - 1):
                for r in range(R):
                    row = tile_row(r, half * HALF + zh, xt)
                    W[pl.ds(out + row, 8), :] = columns(zh, xt, r)
        for zh in range(HALF):
            for xt in range(1, XT - 1):
                for r in range(R):
                    following = finish(zh, xt, r, columns(zh, xt, r))
                    if level < 4:
                        acc[xt] = pack_tile(following, r, zh, acc[xt])
        receive_x(level, half)
        for zh in range(HALF):
            z = half * HALF + zh
            for side, xt, take in ((0, 0, 0), (1, XT - 1, 7)):
                edge = WX[pl.ds((side * NZ + z) * 8, 8), :]
                for r in range(R):
                    halo = HX[level, half, side, pl.ds(r * HALF + zh, 1), :]
                    image = W[pl.ds(out + tile_row(r, z, xt), 8), :]
                    image = image - edge * jnp.broadcast_to(halo, (8, L))
                    following = finish(zh, xt, r, image)
                    if level < 4:
                        XS[level + 1, half, side, pl.ds(r * HALF + zh, 1), :] = (
                            following[take : take + 1]
                        )
        if level < 4:
            send_x(level + 1, half)
        if level < 4:
            for zh in range(HALF):
                for xt, r in tiles:
                    if 0 < xt < XT - 1:
                        continue
                    row = tile_row(r, half * HALF + zh, xt)
                    acc[xt] = pack_tile(F[pl.ds(ahead + row, 8), :], r, zh, acc[xt])
            send_y(level + 1, half, acc)
        if half and level < 4:
            first_rolls(level + 1)

    def combine(a, b, d):
        mask = (sub & d) == 0
        return jnp.where(mask, a, b) + pltpu.roll(jnp.where(mask, b, a), d, 0)

    def gram(level):
        for lev, other, start, pairs in GROUPS:
            if lev != level:
                continue

            def body(step, acc):
                acc = list(acc)
                places = [(2 * step + k, xt) for k in range(2) for xt in range(XT)]
                products(lev, other, pairs, places, acc)
                return tuple(acc)

            fold(list(lax.fori_loop(0, NZ // 2, body, (zero,) * len(pairs))), start)

    for copy in loads[0]:
        copy.wait()
    for copy in loads[3]:
        copy.start()

    packed = []
    for half in range(2):
        def pack_body(step, acc, half=half):
            acc = list(acc)
            for k in range(GROUP):
                zh = step * GROUP + k
                for xt, r in tiles:
                    row = pl.multiple_of(PAD + tile_row(r, half * HALF + zh, xt), 8)
                    tile = F[pl.ds(row, 8), :]
                    acc[xt] = pack_tile(tile, r, zh, acc[xt])
                    for side, where, take in ((0, 0, 0), (1, XT - 1, 7)):
                        if xt == where:
                            XS[0, half, side, pl.ds(r * HALF + zh, 1), :] = tile[take : take + 1]
            return tuple(acc)

        packed.append(lax.fori_loop(0, HALF // GROUP, pack_body, (zero,) * XT))
    pl.semaphore_wait(barrier, len(hello) + len(inner_peers) + len(outer_peers))
    for half in range(2):
        send_x(0, half)
        send_y(0, half, packed[half])

    for copy in loads[1] + loads[2]:
        copy.wait()

    def prepare(z, carry):
        stores = []
        for xt in range(XT):
            row = pl.multiple_of(z * BX + 8 * xt, 8)
            stores.append((C6, row, C6[pl.ds(row, 8), :] + 6.0))
            for side, where, inside, ends in (
                (0, 0, sub != 0, first_x), (1, XT - 1, sub != 7, last_x)
            ):
                if xt == where:
                    w = WM[pl.ds(side * WR + row, 8), :]
                    stores.append((WM, side * WR + row, jnp.where(inside, w, 0.0)))
                    at = pl.multiple_of((side * NZ + z) * 8, 8)
                    stores.append((WX, at, jnp.where(inside | ends, 0.0, w)))
            low = WM[pl.ds(2 * WR + row, 8), :]
            high = WM[pl.ds(3 * WR + row, 8), :]
            edge = jnp.where((lane == 0) & jnp.logical_not(first_y), low, 0.0)
            edge = jnp.where((lane == L - 1) & jnp.logical_not(last_y), high, edge)
            stores.append((WE, row, edge))
            stores.append((WM, 2 * WR + row, jnp.where(lane == 0, 0.0, low)))
            stores.append((WM, 3 * WR + row, jnp.where(lane == L - 1, 0.0, high)))
        for ref, at, value in stores:
            ref[pl.ds(at, 8), :] = value
        return carry

    lax.fori_loop(0, NZ, prepare, 0)
    for xt in range(XT):
        WM[pl.ds(4 * WR + 8 * xt, 8), :] = zero
        WM[pl.ds(5 * WR + (NZ - 1) * BX + 8 * xt, 8), :] = zero
    first_rolls(0)
    bulk(0)
    for copy in loads[3]:
        copy.wait()
    for level in range(5):
        for half in range(2):
            correct(level, half)
        if level < 4:
            bulk(level + 1, level - 1)
            sent(level)
    gram(3)

    for q in range(USED, LANES, 8):
        RED[pl.ds(q, 8), :] = zero
    total = lax.dot_general(
        jnp.ones((8, L), jnp.float32), RED[...], (((1,), (1,)), ((), ())),
        precision=lax.Precision.HIGHEST, preferred_element_type=jnp.float32,
    )

    pending = []

    def exchange(total, buffer, peers, send_sems, recv_sems):
        buffer[pl.ds(0, 8), :] = total
        copies = []
        for k, peer in enumerate(peers):
            copy = pltpu.make_async_remote_copy(
                src_ref=buffer.at[pl.ds(0, 2)], dst_ref=buffer.at[pl.ds(8 + 2 * k, 2)],
                send_sem=send_sems.at[k], recv_sem=recv_sems.at[k],
                device_id=peer, device_id_type=MESH,
            )
            copy.start()
            copies.append(copy)
        own = jnp.where(sub < 2, total, 0.0)
        if not pending:
            sent(4)
        for copy in copies:
            copy.wait_recv()
        parts = [own]
        for at in range(0, 2 * len(peers), 8):
            part = buffer[pl.ds(8 + at, 8), :]
            left = 2 * len(peers) - at
            parts.append(part if left >= 8 else jnp.where(sub < left, part, 0.0))
        while len(parts) > 1:
            parts = [
                parts[k] + parts[k + 1] if k + 1 < len(parts) else parts[k]
                for k in range(0, len(parts), 2)
            ]
        pending.extend(copies)
        total = parts[0]
        for d in (2, 4):
            total = total + pltpu.roll(total, d, 0)
        return total

    total = jnp.where((sub & 1) == 0, total[:, :L], total[:, L:])
    total = exchange(total, RA, inner_peers, sa, ra)
    total = exchange(total, RB, outer_peers, sb, rb)
    swapped = pltpu.roll(total, 1, 0)
    even_row = (sub & 1) == 0
    total = [jnp.where(even_row, total, swapped), jnp.where(even_row, swapped, total)]

    def entry(p):
        return jnp.broadcast_to(total[p // L][:, p % L : p % L + 1], (8, L))

    order = 16
    A = {}
    for i in range(order):
        for j in range(i + 1):
            A[i, j] = entry(TABLE[(i // R, i % R, j // R, j % R)])
    rhs = []
    for i in range(order):
        column = [entry(TABLE[(i // R, i % R, 4, r)]) for r in range(R)]
        rhs.append(
            jnp.where(sub == 0, column[0],
                      jnp.where(sub == 1, column[1],
                                jnp.where(sub == 2, column[2], column[3])))
        )
    lower, inverse = {}, []
    for k in range(order):
        inv = 1.0 / A[k, k]
        inverse.append(inv)
        for i in range(k + 1, order):
            lower[i, k] = A[i, k] * inv
        for i in range(k + 1, order):
            for j in range(k + 1, i + 1):
                A[i, j] = A[i, j] - lower[i, k] * A[j, k]
            rhs[i] = rhs[i] - lower[i, k] * rhs[k]
    coeffs = [None] * order
    for k in range(order - 1, -1, -1):
        value = rhs[k] * inverse[k]
        for i in range(order - 1, k, -1):
            value = value - lower[i, k] * coeffs[i]
        coeffs[k] = value
        for r in range(R):
            CS[pl.ds((r * order + k) * 8, 8), :] = jnp.broadcast_to(value[r : r + 1], (8, L))
    for copy in pending:
        copy.wait_send()


UPDATE_STEPS = 8


def update(F, W, CS, sol_hbm, res_hbm, sol, res, sems):
    planes = NZ // UPDATE_STEPS

    def writes(step):
        where = (slice(None), pl.ds(step * planes, planes))
        return [
            pltpu.make_async_copy(source.at[where], target.at[where], sems.at[k, step])
            for k, (source, target) in enumerate(((sol, sol_hbm), (res, res_hbm)))
        ]

    def body(step, carry):
        def plane(k, carry):
            z = step * planes + k
            sums = []
            for r in range(R):
                for xt in range(XT):
                    row = pl.multiple_of((r * NZ + z) * BX + 8 * xt, 8)
                    sums.append([F[pl.ds(f * FS + PAD + row, 8), :] for f in range(2)])
            for i in range(16):
                coef = [CS[pl.ds((r * 16 + i) * 8, 8), :] for r in range(R)]
                for xt in range(XT):
                    row = pl.multiple_of(((i % R) * NZ + z) * BX + 8 * xt, 8)
                    basis = F[pl.ds((i // R + 1) * FS + PAD + row, 8), :]
                    image = W[pl.ds((i // R) * FR + row, 8), :]
                    for r in range(R):
                        both = sums[r * XT + xt]
                        both[0] = both[0] + coef[r] * basis
                        both[1] = both[1] - coef[r] * image
            for r in range(R):
                for xt in range(XT):
                    sol[r, z, pl.ds(8 * xt, 8), :] = sums[r * XT + xt][0]
                    res[r, z, pl.ds(8 * xt, 8), :] = sums[r * XT + xt][1]
            return carry

        lax.fori_loop(0, planes, plane, 0)
        for copy in writes(step):
            copy.start()
        return carry

    lax.fori_loop(0, UPDATE_STEPS, body, 0)
    for step in range(UPDATE_STEPS):
        for copy in writes(step):
            copy.wait()


def on_device(gx_size, gy_size, right_side, start_field, center, weights):
    inner = min(8, gx_size // 2)
    outer = gx_size // inner
    dma = pltpu.SemaphoreType.DMA
    f32 = jnp.float32
    flat = lambda a: a.reshape(-1, L)
    held = pltpu.MemorySpace.VMEM
    rows_for = lambda devices: 8 + (2 * devices + 5) // 8 * 8
    shape = lambda *dims: jax.ShapeDtypeStruct(dims, f32)
    in_hbm = lambda a: pltpu.with_memory_space_constraint(flat(a), pltpu.HBM)
    fields, images, coeffs = pl.pallas_call(
        functools.partial(kernel, gx_size, gy_size, inner),
        out_shape=[shape(5 * FS, L), shape(4 * FR, L), shape(64 * 8, L)],
        in_specs=[pl.BlockSpec(memory_space=pltpu.HBM)] * 4,
        out_specs=[pl.BlockSpec(memory_space=held)] * 3,
        scratch_shapes=[
            pltpu.VMEM((FR, L), f32),
            pltpu.VMEM((WR, L), f32),
            pltpu.VMEM((6 * WR, L), f32),
            pltpu.VMEM((WR, L), f32),
            pltpu.VMEM((2 * NZ * 8, L), f32),
            pltpu.VMEM((5, 2, 2, R * HALF, L), f32),
            pltpu.VMEM((5, 2, 2, BX, L), f32),
            pltpu.VMEM((5, 2, 2, R * HALF, L), f32),
            pltpu.VMEM((5, 2, BX, L), f32),
            pltpu.VMEM((2 * 2 * GROUP * R * XT * 8, L), f32),
            pltpu.VMEM((8 * USED, L), f32),
            pltpu.VMEM((LANES, L), f32),
            pltpu.VMEM((rows_for(inner), L), f32),
            pltpu.VMEM((rows_for(outer * gy_size), L), f32),
            dma((4, 6)),
            dma((5, 2, 2)), dma((5, 2, 2)), dma((5, 2, 2)), dma((5, 2, 2)),
            dma((inner,)), dma((inner,)),
            dma((outer * gy_size,)), dma((outer * gy_size,)),
        ],
        compiler_params=pltpu.CompilerParams(
            collective_id=0, has_side_effects=True, vmem_limit_bytes=32 * 1024 * 1024,
        ),
    )(in_hbm(right_side), in_hbm(start_field), in_hbm(center), in_hbm(weights))
    return pl.pallas_call(
        update,
        out_shape=[shape(R, NZ, BX, L)] * 2,
        in_specs=[pl.BlockSpec(memory_space=held)] * 3,
        out_specs=[pl.BlockSpec(memory_space=pltpu.HBM)] * 2,
        scratch_shapes=[pltpu.VMEM((R, NZ, BX, L), f32)] * 2 + [dma((2, UPDATE_STEPS))],
        compiler_params=pltpu.CompilerParams(vmem_limit_bytes=16 * 1024 * 1024),
    )(fields, images, coeffs)


def solution(mesh):
    gx_size, gy_size = mesh.shape["gx"], mesh.shape["gy"]
    return jax.shard_map(
        functools.partial(on_device, gx_size, gy_size),
        mesh=mesh,
        in_specs=(
            P(None, None, "gx", "gy"),
            P(None, None, "gx", "gy"),
            P(None, "gx", "gy"),
            P(None, None, "gx", "gy"),
        ),
        out_specs=(P(None, None, "gx", "gy"), P(None, None, "gx", "gy")),
        check_vma=False,
    )
```
